256 devices in a mesh: body: 8 (over x, core), cont: 32 (over z, y).
Axes of the slice: x: 4, y: 4, z: 8, core: 2. Of those that a mesh axis runs over, the one named last changes fastest.
Arguments:
- jacobian: bfloat16 [8, 960, 3, 64, 384], P('body', 'cont'), may hold values from -0.1875 to 0.1875
- contact_block_row: int32 [8, 960], P('body', 'cont'), may hold values from 0 to 79
- block_col: int32 [8, 960], P('body', 'cont'), may hold values from 0 to 159, as said below
- live_count: int32 [32, 80], P('cont', 'body'), may hold values from 1 to 64, as said below
- warm_start: float32 [3, 32, 5120], P(None, 'cont', 'body'), may hold values from -3 to 3
- step_size: float32 [3, 32, 5120], P(None, 'cont', 'body'), may hold values from 0.04 to 0.2
- bias: float32 [32, 5120], P('cont', 'body'), may hold values from -6 to 6
- friction: float32 [32, 5120], P('cont', 'body'), may hold values from 0.2 to 0.9
- free_velocity: float32 [8, 160, 384], P('body', 'cont'), may hold values from -6 to 6
- inv_mass: float32 [8, 160, 384], P('body', 'cont'), may hold values from 0.25 to 2
Outputs:
- impulse: float32 [3, 32, 5120], P(None, 'cont', 'body')
- velocity: float32 [8, 160, 384], P('body', 'cont')
The draws below stay inside these ranges and needn't reach their ends.
Inputs may be any that keep to these rules, and one draw needn't show every extreme that they name: `block_col`: of the 30 blocks of one device (fixed b, q // 30 fixed), at most 3 name body blocks whose index // 5 is the same owner; in each body group one owner is named by exactly 3 blocks of every device of the group. `live_count`: the counts of contact group c are drawn evenly between 1 + (31 - c) * 63 // 31 and 64, so every block of contact group 0 has all 64 contacts live.
All inputs are finite; a program needn't handle non-finite values.
Results may differ from the reference program's by a relative error of at most 0.002.
Values may be sent and summed in bfloat16 or wider, within the bound.
A program may use at most 64 MiB of HBM per device.

```python
import math
import jax
import jax.numpy as jnp
from jax import lax

CONTACTS_IN_BLK = 64
BODIES_PER_BLOCK = 64
SWEEPS = 3
SLOTS = 30
BB_DEV = 5
DEVICE_CBLOCKS = 10
BB_GRP = 160
GROUP_CBLOCKS = 80
CON_GRP = 5120
NONZERO_SLOTS = 960
CAP = 3
N_BODY = 8
N_CONT = 32


def owner_order(sub_key):
    return jax.random.permutation(sub_key, N_CONT)


def draw_block_col(key, part):
    key_rank, key_jitter, key_order, key_within = jax.random.split(key, 4)
    tickets = N_CONT * CAP
    ticket_ids = jnp.arange(tickets, dtype=jnp.int32)
    owner_ids = ticket_ids // CAP
    copy_ids = ticket_ids % CAP
    spacing = max(1, N_CONT // (2 * CAP))
    owner_rank = jax.vmap(owner_order)(jax.random.split(key_rank, N_BODY)).astype(jnp.int32)
    ticket_rank = owner_rank[:, owner_ids][:, None, :]
    jitter = jax.random.randint(key_jitter, (N_BODY, N_CONT, N_CONT), 0, 2, dtype=jnp.int32)[:, :, owner_ids]
    ticket_level = ticket_rank + copy_ids[None, None, :] * spacing + jitter
    ticket_level = jnp.where(ticket_rank == 0, -1, ticket_level)
    ticket_score = (ticket_level + 1) * tickets + ticket_ids[None, None, :]
    chosen = jnp.argsort(ticket_score, axis=-1, stable=True)[:, :, :SLOTS]
    chosen_owner = owner_ids[chosen]
    shuffled = jax.random.permutation(key_order, chosen_owner, axis=2, independent=True)
    within = jax.random.randint(key_within, (N_BODY, N_CONT, SLOTS), 0, BB_DEV, dtype=jnp.int32)
    return (shuffled * BB_DEV + within).reshape(N_BODY, N_CONT * SLOTS).astype(jnp.int32)


def draw_live_count(key, part):
    level_index = jnp.arange(N_CONT, dtype=jnp.int32)[:, None]
    lowest_value = 1 + (N_CONT - 1 - level_index) * (CONTACTS_IN_BLK - 1) // max(1, N_CONT - 1)
    lowest_value = jnp.broadcast_to(lowest_value, (N_CONT, N_BODY * DEVICE_CBLOCKS))
    return jax.random.randint(key, (N_CONT, N_BODY * DEVICE_CBLOCKS), lowest_value, CONTACTS_IN_BLK + 1, dtype=jnp.int32)


def touch_ends(values, key, low, top_value):
    extent = values.shape
    spot = [jax.random.randint(jax.random.fold_in(key, axis), (), 0, extent[axis]) for axis in range(len(extent))]
    values = values.at[tuple(spot)].set(low)
    longest = extent.index(max(extent))
    spot[longest] = (spot[longest] + 1) % extent[longest]
    return values.at[tuple(spot)].set(top_value)


def level_of(own_key, extent, cuts, low, largest):
    loudness, own = 1.0, jax.random.fold_in(own_key, 6)
    for axis_at, shards_of in cuts:
        steps = jnp.exp(jax.random.uniform(jax.random.fold_in(own, axis_at), (shards_of,), jnp.float32, low / len(cuts), largest / len(cuts)))
        loudness = loudness * jnp.repeat(steps, extent[axis_at] // shards_of).reshape([-1 if axis == axis_at else 1 for axis in range(len(extent))])
    return loudness


def scatter_about(own_key, dims, spread, reach, cuts=(), kind=jnp.bfloat16):
    gain = level_of(own_key, dims, cuts, -0.22, 0.18) if cuts else 1.0
    result = jax.random.normal(own_key, dims, jnp.float32) * spread * gain
    return jnp.minimum(jnp.maximum(result, -reach), reach).astype(kind)


def setup_inputs(seed: int = 0) -> dict:
    streams_of = jax.random.split(jax.random.key(seed), 11)
    return {
        "jacobian": scatter_about(streams_of[0], (N_BODY, NONZERO_SLOTS, 3, CONTACTS_IN_BLK, 6 * BODIES_PER_BLOCK), (18 * BODIES_PER_BLOCK) ** -0.5, 0.1875, ((0, 8), (1, 32))),
        "contact_block_row": touch_ends(jax.random.randint(streams_of[1], (N_BODY, NONZERO_SLOTS), 0, GROUP_CBLOCKS), jax.random.fold_in(streams_of[1], 1), 0, GROUP_CBLOCKS - 1).astype(jnp.int32),
        "block_col": draw_block_col(jax.random.fold_in(streams_of[10], 71), 0),
        "live_count": draw_live_count(jax.random.fold_in(streams_of[10], 71), 0),
        "warm_start": scatter_about(streams_of[4], (3, N_CONT, CON_GRP), 0.5, 3.0, ((1, 32), (2, 8)), jnp.float32),
        "step_size": jnp.clip(jnp.exp(math.log(0.2) - 1.609438 * jax.random.uniform(streams_of[5], (3, N_CONT, CON_GRP), jnp.float32) ** level_of(streams_of[5], (3, N_CONT, CON_GRP), ((1, 32), (2, 8)), -0.2, 0.2)), 0.04, 0.2),
        "bias": scatter_about(streams_of[6], (N_CONT, CON_GRP), 1.0, 6.0, ((0, 32), (1, 8)), jnp.float32),
        "friction": jnp.clip(0.2 + 0.7 * jax.random.uniform(streams_of[7], (N_CONT, CON_GRP), jnp.float32) ** level_of(streams_of[7], (N_CONT, CON_GRP), ((0, 32), (1, 8)), -0.2, 0.2), 0.2, 0.9),
        "free_velocity": scatter_about(streams_of[8], (N_BODY, BB_GRP, 6 * BODIES_PER_BLOCK), 1.0, 6.0, ((0, 8), (1, 32)), jnp.float32),
        "inv_mass": jnp.clip(jnp.exp(math.log(2.0) - 2.0794415 * jax.random.uniform(streams_of[9], (N_BODY, BB_GRP, 6 * BODIES_PER_BLOCK), jnp.float32) ** level_of(streams_of[9], (N_BODY, BB_GRP, 6 * BODIES_PER_BLOCK), ((0, 8), (1, 32)), -0.2, 0.2)), 0.25, 2.0),
    }


def reference(jacobian, contact_block_row, block_col, live_count, warm_start, step_size, bias, friction, free_velocity, inv_mass):
    slot_total = N_CONT * SLOTS
    contact_block_count = N_BODY * DEVICE_CBLOCKS
    body_blocks = N_CONT * BB_DEV
    exact_mode = lax.Precision.HIGHEST
    group_of_slot = jnp.arange(slot_total, dtype=jnp.int32) // SLOTS
    slot_position = jnp.arange(CONTACTS_IN_BLK, dtype=jnp.int32)
    active_mask = (slot_position[None, None, :] < live_count[:, :, None]).astype(jnp.float32)
    active_mask = active_mask.reshape(N_CONT, contact_block_count * CONTACTS_IN_BLK)
    zero_part = jnp.zeros_like(bias)
    normal_shift = jnp.stack([bias, zero_part, zero_part])

    def forces(present_impulse):
        rounded_result = present_impulse.astype(jnp.bfloat16).reshape(3, N_CONT, contact_block_count, CONTACTS_IN_BLK)

        def one_group(pieces):
            blocks_g, row_ids, col_ids = pieces
            slot_imp = rounded_result[:, group_of_slot, row_ids, :].astype(jnp.float32)
            slot_force = jnp.einsum("sijd,isj->sd", blocks_g.astype(jnp.float32), slot_imp, precision=exact_mode)
            return jnp.zeros((body_blocks, 6 * BODIES_PER_BLOCK), jnp.float32).at[col_ids].add(slot_force)

        return lax.map(one_group, (jacobian, contact_block_row, block_col))

    def contact_velocity(velocity_now):
        rounded_result = velocity_now.astype(jnp.bfloat16)

        def one_group(running, pieces):
            blocks_g, row_ids, col_ids, group_vel = pieces
            slot_vel = group_vel[col_ids].astype(jnp.float32)
            slot_local = jnp.einsum("sijd,sd->sij", blocks_g.astype(jnp.float32), slot_vel, precision=exact_mode)
            return running.at[group_of_slot, row_ids].add(slot_local), None

        starting_impulse = jnp.zeros((N_CONT, contact_block_count, 3, CONTACTS_IN_BLK), jnp.float32)
        summed_rows, _ = lax.scan(one_group, starting_impulse, (jacobian, contact_block_row, block_col, rounded_result))
        return jnp.transpose(summed_rows, (2, 0, 1, 3)).reshape(3, N_CONT, contact_block_count * CONTACTS_IN_BLK)

    present_impulse = warm_start * active_mask
    for sweep_no in range(SWEEPS):
        velocity_now = free_velocity + inv_mass * forces(present_impulse)
        local_velocity = contact_velocity(velocity_now)
        trial_step = present_impulse - step_size * (local_velocity + normal_shift)
        normal = jnp.maximum(trial_step[0], 0.0)
        cone_limit = friction * normal
        tangent = jnp.clip(trial_step[1:], -cone_limit, cone_limit)
        present_impulse = jnp.concatenate([normal[None], tangent], axis=0) * active_mask
    velocity_final = free_velocity + inv_mass * forces(present_impulse)
    return (present_impulse, velocity_final)
```

```python
import jax
import jax.numpy as jnp
from jax import lax
from jax.experimental import pallas as pl
from jax.experimental.pallas import tpu as pltpu
from jax.sharding import PartitionSpec as P

MESH = pl.DeviceIdType.MESH
SWEEPS = 3
SLOTS = 30
F32, BF16, I32 = jnp.float32, jnp.bfloat16, jnp.int32


def iota(shape, dim):
    return lax.broadcasted_iota(I32, shape, dim)


def half_turn(x):
    return pltpu.roll(x, 64, axis=x.ndim - 1)


def split(x):
    hi = x.astype(BF16)
    mid = (x - hi.astype(F32)).astype(BF16)
    return hi, mid


def mm(a, b):
    return jnp.dot(a, b, preferred_element_type=F32)


def kernel(
    jac_in, row_in, col_in, live_in, warm_in, step_in, bias_in, fric_in, free_in, mass_in,
    imp_out, vel_out,
    jac, rowv, colv, livev, warm, step, bias, fric, free, mass,
    ids, pick, owner_one, slot_one, row_one, gather_one,
    imp_a, imp_b, free16, mass16,
    tab_send, tab_recv, con_send, con_recv, meta_send, meta_recv,
    force_send, force_recv, vel_send, vel_recv, loc_send, loc_recv,
    jac_sem, in_sem, tab_s, tab_r, con_s, con_r, meta_s, meta_r,
    force_s, force_r, vel_s, vel_r, loc_s, loc_r,
):
    b, c = lax.axis_index("body"), lax.axis_index("cont")
    x, core, z, y = b // 2, b % 2, c // 4, c % 4

    def cont_peer(k):
        i, j = k // 4, k % 4
        dz = 4 + (1 - 2 * (i % 2)) * ((i + 1) // 2)
        dy = 2 + (1 - 2 * (j % 2)) * ((j + 1) // 2)
        return ((z + dz) % 8) * 4 + (y + dy) % 4

    body_peers = [
        ((x + dx) % 4) * 2 + (core + dc) % 2
        for dx, dc in ((2, 1), (2, 0), (1, 1), (3, 1), (1, 0), (3, 0), (0, 1))
    ]

    def over_cont(go):
        def one(k, carry):
            go(cont_peer(k))
            return carry

        lax.fori_loop(0, 31, one, 0)

    def send_body(src, dst, ssem, rsem):
        for p in body_peers:
            pltpu.make_async_remote_copy(
                src_ref=src, dst_ref=dst, send_sem=ssem, recv_sem=rsem,
                device_id={"body": p}, device_id_type=MESH,
            ).start()

    def drain(ref, sem):
        pltpu.make_async_copy(ref, ref, sem).wait()

    bar = pltpu.get_barrier_semaphore()
    over_cont(lambda p: pl.semaphore_signal(bar, inc=1, device_id={"cont": p}, device_id_type=MESH))
    for p in body_peers:
        pl.semaphore_signal(bar, inc=1, device_id={"body": p}, device_id_type=MESH)

    pairs = (
        (row_in, rowv), (col_in, colv), (live_in, livev), (warm_in, warm), (step_in, step),
        (bias_in, bias), (fric_in, fric), (free_in, free), (mass_in, mass),
    )
    small = [pltpu.make_async_copy(s, d, in_sem.at[n]) for n, (s, d) in enumerate(pairs)]
    for cp in small:
        cp.start()
    blocks = [
        pltpu.make_async_copy(jac_in.at[pl.ds(n * 6, 6)], jac.at[pl.ds(n * 6, 6)], jac_sem.at[n])
        for n in range(5)
    ]
    for cp in blocks:
        cp.start()
    for cp in small:
        cp.wait()

    lane16 = iota((16, 128), 1)
    low16 = lane16 < 64
    lane8 = iota((8, 128), 1)
    low8 = lane8 < 64

    def rows_of(get):
        parts = [get(p).astype(F32) for p in range(5)]
        return jnp.concatenate(parts + [jnp.zeros((3, 128), F32)], axis=0)

    def planes(ref):
        w0, w1, w2 = [rows_of(lambda p, i=i: ref[i, 0:1, p * 128:(p + 1) * 128]) for i in range(3)]
        even = jnp.where(low8, w0, half_turn(w1))
        odd = jnp.where(low8, half_turn(w0), w1)
        return jnp.concatenate([even, odd], 0), jnp.concatenate([w2, half_turn(w2)], 0)

    def high_plane(ref):
        f = rows_of(lambda p: ref[0:1, p * 128:(p + 1) * 128])
        return jnp.concatenate([half_turn(f), f], 0)

    sub10 = iota((16, 10), 0)
    block_of_row = 2 * (sub10 & 7) + (sub10 >> 3)
    live_row = jnp.sum(
        jnp.where(iota((16, 10), 1) == block_of_row, livev[...].astype(F32), 0.0), axis=1, keepdims=True
    )
    active = (lane16 & 63).astype(F32) < live_row
    wa, wb = planes(warm)
    sa, sb = planes(step)
    tab_send[0] = jnp.where(active, wa, 0.0)
    tab_send[1] = jnp.where(low16, jnp.where(active, wb, 0.0), jnp.where(active, high_plane(fric), -1.0))
    con_send[0] = sa
    con_send[1] = jnp.where(low16, sb, high_plane(bias))

    ids[0:1, :] = jnp.where(iota((1, 128), 1) < 32, 9999, 0)
    ids[1:2, :] = jnp.where(iota((1, 128), 1) < 32, 10000, 0)
    ids[0:1, 0:SLOTS] = rowv[...]
    ids[1:2, 0:SLOTS] = colv[...]
    lane1 = iota((1, 128), 1)
    row_l = ids[0:1, :]
    dev = (row_l * 52429) >> 19
    kk = row_l - 10 * dev
    place_l = jnp.where(
        lane1 < SLOTS, dev * 16 + (kk & 1) * 8 + (kk >> 1), jnp.where(lane1 < 32, 9999, 0)
    ).astype(F32)
    col_l = ids[1:2, :]
    owner_i = (col_l * 52429) >> 18
    within_l = (col_l - 5 * owner_i).astype(F32)
    owner_l = owner_i.astype(F32)

    sub32, lane32 = iota((32, 128), 0), iota((32, 128), 1)

    def down(v):
        return jnp.sum(jnp.where(sub32 == lane32, jnp.broadcast_to(v, (32, 128)), 0.0), axis=1, keepdims=True)

    place_s, owner_s, within_s = down(place_l), down(owner_l), down(within_l)
    rank_l = jnp.sum(
        jnp.where((owner_s == owner_l) & (sub32 < lane32) & (lane32 < 32), 1.0, 0.0), axis=0, keepdims=True
    )
    con_send[2] = jnp.broadcast_to(pltpu.roll(jnp.broadcast_to(place_l, (8, 128)), (b % 4) * 32, axis=1)[0:1], (16, 128))

    def four_times(v):
        v = jnp.broadcast_to(v, (8, 128))
        v = v + pltpu.roll(v, 32, axis=1)
        return (v + pltpu.roll(v, 64, axis=1))[0:1]

    owner4, rank4 = four_times(owner_l), four_times(rank_l)
    sub = iota((288, 1), 0)
    o_row = jnp.where(sub < 256, sub >> 3, sub - 256)
    m_row = jnp.where(sub < 256, sub & 7, 8)
    r_row = jnp.where(m_row < 3, 0, jnp.where(m_row < 6, 1, 2))
    c_row = m_row - 3 * r_row
    hit = (owner4 == o_row.astype(F32)) & (rank4 == r_row.astype(F32))
    for tile in range(2):
        q = (iota((1, 128), 1) >> 5) + 4 * tile
        cq = jnp.where(q < 3, q, jnp.where(q < 6, q - 3, -1))
        pick[:, tile * 128:(tile + 1) * 128] = jnp.where(hit & (cq == c_row), 1.0, 0.0).astype(BF16)
    sub96 = iota((96, 1), 0)
    c96 = (sub96 >> 5).astype(F32)
    within96 = jnp.concatenate([within_s] * 3, axis=0)
    target96 = jnp.concatenate([owner_s * 16 + within_s] * 3, axis=0) + 5 * c96
    mark = jnp.where(iota((96, 128), 1).astype(F32) == within96 + 5 * c96, 1.0, 0.0).astype(BF16)
    mv = mm(pick[:, 0:96], mark)
    meta_send[:, 0:8, :] = mv[0:256].reshape(32, 8, 128)
    meta_send[:, 8:9, :] = mv[256:288].reshape(32, 1, 128)
    gather_one[...] = jnp.where(iota((96, 512), 1).astype(F32) == target96, 1.0, 0.0).astype(BF16)
    slot_one[...] = jnp.where(lane32.astype(F32) == place_s, 1.0, 0.0).astype(BF16)
    for src, dst in ((free, free16), (mass, mass16)):
        v = src[0]
        dst[...] = jnp.concatenate(
            [v[:, 0:128], v[:, 128:256], v[:, 256:384], jnp.zeros((1, 128), F32)], axis=0
        )

    pl.semaphore_wait(bar, 38)

    send_body(tab_send, tab_recv.at[b], tab_s, tab_r)
    tab_recv[b] = tab_send[...]
    send_body(con_send, con_recv.at[b], con_s, con_r)
    con_recv[b] = con_send[...]

    def send_meta(p):
        pltpu.make_async_remote_copy(
            src_ref=meta_send.at[p], dst_ref=meta_recv.at[c], send_sem=meta_s, recv_sem=meta_r,
            device_id={"cont": p}, device_id_type=MESH,
        ).start()

    over_cont(send_meta)
    meta_recv[c] = meta_send[c]

    drain(tab_recv.at[pl.ds(0, 7)], tab_r)
    imp_a[...] = tab_recv[:, 0].reshape(128, 128)
    imp_b[...] = tab_recv[:, 1].reshape(128, 128)
    for cp in blocks:
        cp.wait()

    low32 = lane32 < 64

    def forces():
        a, bb = imp_a[...].astype(BF16), imp_b[...].astype(BF16)
        ya, yb = mm(slot_one[...], a), mm(slot_one[...], bb)
        turned = half_turn(ya)
        pattern = jnp.concatenate(
            [ya, jnp.where(low32, yb, turned), jnp.where(low32, turned, half_turn(yb))], axis=1
        ).astype(BF16)
        halves = []
        row = iota((16, 768), 0)
        lane = iota((16, 768), 1) // 192
        for h in range(2):
            rep = jnp.concatenate([pattern[16 * h:16 * h + 16]] * 2, axis=1)
            acc = jnp.zeros((16, 384), F32)
            for g in range(0, 16, 4):
                s = 16 * h + g
                n = min(4, SLOTS - s)
                lhs = jnp.where(lane + g == row, rep, jnp.zeros_like(rep))[:, :n * 192]
                acc = acc + mm(lhs, jac[s:s + n].reshape(n * 192, 384))
            halves.append(acc)
        return jnp.concatenate(halves, axis=0)

    def locals_of(v):
        halves = []
        row = iota((16, 384), 0)
        lane = iota((16, 384), 1) // 192
        for h in range(2):
            acc = jnp.zeros((16, 384), F32)
            for g in range(0, 16, 4):
                s = 16 * h + g
                n = min(4, SLOTS - s)
                o = lax.dot_general(
                    v[16 * h:16 * h + 16], jac[s:s + n].reshape(n * 192, 384),
                    (((1,), (1,)), ((), ())), preferred_element_type=F32,
                )
                for p in range(0, n, 2):
                    acc = acc + jnp.where(lane + (g + p) == row, o[:, p * 192:p * 192 + 384], 0.0)
            halves.append(acc)
        return jnp.concatenate(halves, axis=0)

    def sweep(t, carry):
        hi, mid = split(forces())
        stacked = jnp.concatenate(
            [part[:, n * 128:(n + 1) * 128] for part in (hi, mid) for n in range(3)], axis=0
        )
        packed = mm(pick[:, 0:192], stacked)
        force_send[t, :, 0:8, :] = packed[0:256].reshape(32, 8, 128)
        force_send[t, :, 8:9, :] = packed[256:288].reshape(32, 1, 128)

        def send_force(p):
            pltpu.make_async_remote_copy(
                src_ref=force_send.at[t, p], dst_ref=force_recv.at[t, c], send_sem=force_s.at[t],
                recv_sem=force_r.at[t], device_id={"cont": p}, device_id_type=MESH,
            ).start()

        over_cont(send_force)
        force_recv[t, c] = force_send[t, c]

        @pl.when(t == 0)
        def _():
            drain(meta_recv.at[pl.ds(0, 31)], meta_r)
            meta = jnp.concatenate(
                [meta_recv[:, 0:8, :].reshape(256, 128), meta_recv[:, 8:9, :].reshape(32, 128),
                 jnp.zeros((96, 128), F32)], axis=0
            )
            owner_one[...] = jnp.transpose(meta)[0:16].astype(BF16)
            drain(con_recv.at[pl.ds(0, 7)], con_r)
            lo = con_recv[0, 2] + con_recv[1, 2] + con_recv[2, 2] + con_recv[3, 2]
            hi_ids = con_recv[4, 2] + con_recv[5, 2] + con_recv[6, 2] + con_recv[7, 2]
            sub128 = iota((128, 128), 0).astype(F32)
            row_one[:, 0:128] = jnp.where(sub128 == lo[0:1], 1.0, 0.0).astype(BF16)
            row_one[:, 128:256] = jnp.where(sub128 == hi_ids[0:1], 1.0, 0.0).astype(BF16)

        drain(force_recv.at[t, pl.ds(0, 31)], force_r.at[t])
        got = jnp.concatenate(
            [force_recv[t, :, 0:8, :].reshape(256, 128), force_recv[t, :, 8:9, :].reshape(32, 128),
             jnp.zeros((96, 128), F32)], axis=0
        )
        ghi, gmid = split(got)
        force = mm(owner_one[...], ghi) + mm(owner_one[...], gmid)
        velocity = free16[...] + mass16[...] * force

        @pl.when(t == SWEEPS)
        def _():
            for n in range(3):
                vel_out[0, :, n * 128:(n + 1) * 128] = velocity[n * 5:n * 5 + 5]

        @pl.when(t < SWEEPS)
        def _():
            vel_send[t] = velocity.astype(BF16)

            def send_vel(p):
                pltpu.make_async_remote_copy(
                    src_ref=vel_send.at[t], dst_ref=vel_recv.at[t, c], send_sem=vel_s.at[t],
                    recv_sem=vel_r.at[t], device_id={"cont": p}, device_id_type=MESH,
                ).start()

            over_cont(send_vel)
            vel_recv[t, c] = vel_send[t]
            drain(vel_recv.at[t, pl.ds(0, 31)], vel_r.at[t])
            vs = mm(gather_one[...], vel_recv[t].reshape(512, 128)).astype(BF16)
            v = jnp.concatenate([vs[0:32], vs[32:64], vs[64:96]], axis=1)
            loc = locals_of(v)
            l0, l1, l2 = loc[:, 0:128], loc[:, 128:256], loc[:, 256:384]
            even = (sub32 & 1) == 0
            t2 = half_turn(l2)
            la = jnp.where(even, l0, jnp.where(low32, half_turn(l1), t2))
            lb = jnp.where(even, l1, t2)
            ahi, amid = split(la)
            bhi = lb.astype(BF16).astype(F32)
            loc_send[t, 0] = ahi
            loc_send[t, 1] = amid
            loc_send[t, 2] = jnp.where(low32, bhi, half_turn(lb - bhi)).astype(BF16)
            send_body(loc_send.at[t], loc_recv.at[t, b], loc_s.at[t], loc_r.at[t])
            loc_recv[t, b] = loc_send[t]
            drain(loc_recv.at[t, pl.ds(0, 7)], loc_r.at[t])
            r1 = row_one[...]
            lva = mm(r1, loc_recv[t, :, 0].reshape(256, 128)) + mm(r1, loc_recv[t, :, 1].reshape(256, 128))
            lvb = mm(r1, loc_recv[t, :, 2].reshape(256, 128))
            lvb = lvb + half_turn(lvb)
            low = iota((128, 128), 1) < 64
            fric_high = tab_recv[:, 1].reshape(128, 128)
            step_b = con_recv[:, 1].reshape(128, 128)
            fr = jnp.where(low, half_turn(fric_high), fric_high)
            shift = jnp.where(low, half_turn(step_b), 0.0)
            ta = imp_a[...] - con_recv[:, 0].reshape(128, 128) * (lva + shift)
            tb = imp_b[...] - step_b * lvb
            normal = jnp.where(low, jnp.maximum(ta, 0.0), 0.0)
            lim_a = fr * half_turn(normal)
            lim_b = fr * normal
            live = fr >= 0.0
            new_a = jnp.where(low, normal, jnp.clip(ta, -lim_a, lim_a))
            imp_a[...] = jnp.where(live, new_a, 0.0)
            imp_b[...] = jnp.where(live & low, jnp.clip(tb, -lim_b, lim_b), 0.0)

        return carry

    lax.fori_loop(0, SWEEPS + 1, sweep, 0)

    own_a = imp_a[pl.ds(b * 16, 16), :]
    own_b = imp_b[pl.ds(b * 16, 16), :]
    ae, ao, be, bo = own_a[0:8], own_a[8:16], own_b[0:8], own_b[8:16]
    outs = (
        jnp.where(low8, ae, half_turn(ao)),
        jnp.where(low8, half_turn(ae), ao),
        jnp.where(low8, be, half_turn(bo)),
    )
    for i in range(3):
        for p in range(5):
            imp_out[i, 0:1, p * 128:(p + 1) * 128] = outs[i][p:p + 1]

    drain(tab_recv.at[pl.ds(0, 7)], tab_s)
    drain(con_recv.at[pl.ds(0, 7)], con_s)
    drain(meta_recv.at[pl.ds(0, 31)], meta_s)
    for t in range(SWEEPS + 1):
        drain(force_recv.at[t, pl.ds(0, 31)], force_s.at[t])
        if t < SWEEPS:
            drain(vel_recv.at[t, pl.ds(0, 31)], vel_s.at[t])
            drain(loc_recv.at[t, pl.ds(0, 7)], loc_s.at[t])


def shards(jacobian, row, col, live, warm, step, bias, fric, free, mass):
    dma = pltpu.SemaphoreType.DMA
    passes = SWEEPS + 1
    any_spec = pl.BlockSpec(memory_space=pl.ANY)
    vmem = pl.BlockSpec(memory_space=pltpu.VMEM)
    return pl.pallas_call(
        kernel,
        out_shape=(jax.ShapeDtypeStruct((3, 1, 640), F32), jax.ShapeDtypeStruct((1, 5, 384), F32)),
        in_specs=[any_spec] * 10,
        out_specs=(vmem, vmem),
        scratch_shapes=[
            pltpu.VMEM((SLOTS, 3, 64, 384), BF16),
            pltpu.VMEM((1, SLOTS), I32),
            pltpu.VMEM((1, SLOTS), I32),
            pltpu.VMEM((1, 10), I32),
            pltpu.VMEM((3, 1, 640), F32),
            pltpu.VMEM((3, 1, 640), F32),
            pltpu.VMEM((1, 640), F32),
            pltpu.VMEM((1, 640), F32),
            pltpu.VMEM((1, 5, 384), F32),
            pltpu.VMEM((1, 5, 384), F32),
            pltpu.VMEM((8, 128), I32),
            pltpu.VMEM((288, 256), BF16),
            pltpu.VMEM((16, 384), BF16),
            pltpu.VMEM((32, 128), BF16),
            pltpu.VMEM((128, 256), BF16),
            pltpu.VMEM((96, 512), BF16),
            pltpu.VMEM((128, 128), F32),
            pltpu.VMEM((128, 128), F32),
            pltpu.VMEM((16, 128), F32),
            pltpu.VMEM((16, 128), F32),
            pltpu.VMEM((2, 16, 128), F32),
            pltpu.VMEM((8, 2, 16, 128), F32),
            pltpu.VMEM((3, 16, 128), F32),
            pltpu.VMEM((8, 3, 16, 128), F32),
            pltpu.VMEM((32, 9, 128), F32),
            pltpu.VMEM((32, 9, 128), F32),
            pltpu.VMEM((passes, 32, 9, 128), F32),
            pltpu.VMEM((passes, 32, 9, 128), F32),
            pltpu.VMEM((SWEEPS, 16, 128), BF16),
            pltpu.VMEM((SWEEPS, 32, 16, 128), BF16),
            pltpu.VMEM((SWEEPS, 3, 32, 128), BF16),
            pltpu.VMEM((SWEEPS, 8, 3, 32, 128), BF16),
            dma((5,)), dma((9,)), dma, dma, dma, dma, dma, dma,
            dma((passes,)), dma((passes,)), dma((SWEEPS,)), dma((SWEEPS,)), dma((SWEEPS,)), dma((SWEEPS,)),
        ],
        compiler_params=pltpu.CompilerParams(
            collective_id=0, has_side_effects=True, vmem_limit_bytes=40 << 20
        ),
        name="sweeps",
    )(jacobian.reshape(jacobian.shape[1:]), row, col, live, warm, step, bias, fric, free, mass)


def solution(mesh):
    placed = (
        P("body", "cont", None, None, None),
        P("body", "cont"),
        P("body", "cont"),
        P("cont", "body"),
        P(None, "cont", "body"),
        P(None, "cont", "body"),
        P("cont", "body"),
        P("cont", "body"),
        P("body", "cont", None),
        P("body", "cont", None),
    )
    return jax.shard_map(
        shards,
        mesh=mesh,
        in_specs=placed,
        out_specs=(P(None, "cont", "body"), P("body", "cont", None)),
        check_vma=False,
    )
```

```python
import jax
import jax.numpy as jnp
from jax import lax
from jax.experimental import pallas as pl
from jax.experimental.pallas import tpu as pltpu
from jax.sharding import PartitionSpec as P

MESH = pl.DeviceIdType.MESH
SWEEPS = 3
SLOTS = 30
NEAR = (
    (1, 2), (7, 2), (2, 1), (6, 1), (2, 0), (6, 0), (1, 1), (1, 3), (7, 1), (7, 3), (0, 2),
    (1, 0), (7, 0), (0, 1), (0, 3),
)
F32, BF16, I32 = jnp.float32, jnp.bfloat16, jnp.int32


def iota(shape, dim):
    return lax.broadcasted_iota(I32, shape, dim)


def half_turn(x):
    return pltpu.roll(x, 64, axis=x.ndim - 1)


def split(x):
    hi = x.astype(BF16)
    mid = (x - hi.astype(F32)).astype(BF16)
    return hi, mid


def mm(a, b):
    return jnp.dot(a, b, preferred_element_type=F32)


def kernel(
    jac_in, row_in, col_in, live_in, warm_in, step_in, bias_in, fric_in, free_in, mass_in,
    out,
    jac, rowv, colv, livev, warm, step, bias, fric, free, mass,
    jact, ids, pick, owner_one, slot_one, row_one, gather_one,
    imp_a, imp_b, step_a, step_b, fric48, shift48, home,
    tab_send, tab_recv, con_send, con_recv, meta_send, meta_recv,
    force_send, force_recv, vel_send, vel_recv, loc_send, loc_recv,
    jac_sem, in_sem, home_s, home_r, tab_s, tab_r, con_s, con_r, meta_s, meta_r,
    force_s, force_r, vel_s, vel_r, loc_s, loc_r,
):
    b, c = lax.axis_index("body"), lax.axis_index("cont")
    x, core, z, y = b // 2, b % 2, c // 4, c % 4

    def cont_peer(k):
        i, j = k // 4, k % 4
        dz = 4 + (1 - 2 * (i % 2)) * ((i + 1) // 2)
        dy = 2 + (1 - 2 * (j % 2)) * ((j + 1) // 2)
        return ((z + dz) % 8) * 4 + (y + dy) % 4

    def moved(dz, dy):
        return ((z + dz) % 8) * 4 + (y + dy) % 4

    def antipode(p):
        return ((p // 4 + 4) % 8) * 4 + (p % 4 + 2) % 4

    body_peers = [
        ((x + dx) % 4) * 2 + (core + dc) % 2
        for dx, dc in ((2, 1), (2, 0), (1, 1), (3, 1), (1, 0), (3, 0), (0, 1))
    ]

    def over_cont(go):
        def one(k, carry):
            go(cont_peer(k))
            return carry

        lax.fori_loop(0, 31, one, 0)

    def send_body(src, dst, ssem, rsem):
        for p in body_peers:
            pltpu.make_async_remote_copy(
                src_ref=src, dst_ref=dst, send_sem=ssem, recv_sem=rsem,
                device_id={"body": p}, device_id_type=MESH,
            ).start()

    def drain(ref, sem):
        pltpu.make_async_copy(ref, ref, sem).wait()

    bar = pltpu.get_barrier_semaphore()
    over_cont(lambda p: pl.semaphore_signal(bar, inc=1, device_id={"cont": p}, device_id_type=MESH))
    for p in body_peers:
        pl.semaphore_signal(bar, inc=1, device_id={"body": p}, device_id_type=MESH)

    pairs = (
        (warm_in, warm), (live_in, livev), (row_in, rowv), (col_in, colv), (step_in, step),
        (bias_in, bias), (fric_in, fric), (free_in, free), (mass_in, mass),
    )
    small = [pltpu.make_async_copy(s, d, in_sem.at[n]) for n, (s, d) in enumerate(pairs)]
    for cp in small:
        cp.start()
    blocks = [
        pltpu.make_async_copy(jac_in.at[pl.ds(n * 6, 6)], jac.at[pl.ds(n * 6, 6)], jac_sem.at[n])
        for n in range(5)
    ]
    for cp in blocks:
        cp.start()
    for cp in small[:2]:
        cp.wait()

    lane16 = iota((16, 128), 1)
    low16 = lane16 < 64
    lane8 = iota((8, 128), 1)
    low8 = lane8 < 64

    def rows_of(get):
        parts = [get(p).astype(F32) for p in range(5)]
        return jnp.concatenate(parts + [jnp.zeros((3, 128), F32)], axis=0)

    def planes(ref):
        w0, w1, w2 = [rows_of(lambda p, i=i: ref[i, 0:1, p * 128:(p + 1) * 128]) for i in range(3)]
        even = jnp.where(low8, w0, half_turn(w1))
        odd = jnp.where(low8, half_turn(w0), w1)
        return jnp.concatenate([even, odd], 0), jnp.concatenate([w2, half_turn(w2)], 0)

    def high_plane(ref):
        f = rows_of(lambda p: ref[0:1, p * 128:(p + 1) * 128])
        return jnp.concatenate([half_turn(f), f], 0)

    sub10 = iota((16, 10), 0)
    block_of_row = 2 * (sub10 & 7) + (sub10 >> 3)
    live_row = jnp.sum(
        jnp.where(iota((16, 10), 1) == block_of_row, livev[...].astype(F32), 0.0), axis=1, keepdims=True
    )
    active = (lane16 & 63).astype(F32) < live_row
    wa, wb = planes(warm)
    wa, wb = jnp.where(active, wa, 0.0), jnp.where(active & low16, wb, 0.0)
    tab_send[0] = wa.astype(BF16)
    tab_send[1] = wb.astype(BF16)
    pl.semaphore_wait(bar, 38)
    send_body(tab_send, tab_recv.at[b], tab_s, tab_r)
    tab_recv[b] = tab_send[...]

    for cp in small[2:]:
        cp.wait()
    sa, sb = planes(step)
    con_send[0] = wa
    con_send[1] = jnp.where(low16, wb, jnp.where(active, high_plane(fric), -1.0))
    con_send[2] = sa
    con_send[3] = jnp.where(low16, sb, high_plane(bias))

    ids[0:1, :] = jnp.where(iota((1, 128), 1) < 32, 9999, 0)
    ids[1:2, :] = jnp.where(iota((1, 128), 1) < 32, 10000, 0)
    ids[0:1, 0:SLOTS] = rowv[...]
    ids[1:2, 0:SLOTS] = colv[...]
    lane1 = iota((1, 128), 1)
    row_l = ids[0:1, :]
    dev = (row_l * 52429) >> 19
    kk = row_l - 10 * dev
    place_l = jnp.where(
        lane1 < SLOTS, dev * 16 + (kk & 1) * 8 + (kk >> 1), jnp.where(lane1 < 32, 9999, 0)
    ).astype(F32)
    col_l = ids[1:2, :]
    owner_i = (col_l * 52429) >> 18
    within_l = (col_l - 5 * owner_i).astype(F32)
    owner_l = owner_i.astype(F32)

    sub32, lane32 = iota((32, 128), 0), iota((32, 128), 1)

    def down(v):
        return jnp.sum(jnp.where(sub32 == lane32, jnp.broadcast_to(v, (32, 128)), 0.0), axis=1, keepdims=True)

    place_s, owner_s, within_s = down(place_l), down(owner_l), down(within_l)
    rank_l = jnp.sum(
        jnp.where((owner_s == owner_l) & (sub32 < lane32) & (lane32 < 32), 1.0, 0.0), axis=0, keepdims=True
    )
    place8 = jnp.broadcast_to(place_l, (8, 128))
    con_send[4, 0:8, :] = pltpu.roll(jnp.where(lane8 < 16, place8, 0.0), b * 16, axis=1)
    con_send[4, 8:16, :] = pltpu.roll(jnp.where((lane8 >= 16) & (lane8 < 32), place8, 0.0), (b * 16 + 112) % 128, axis=1)

    def four_times(v):
        v = jnp.broadcast_to(v, (8, 128))
        v = v + pltpu.roll(v, 32, axis=1)
        return (v + pltpu.roll(v, 64, axis=1))[0:1]

    owner4, rank4 = four_times(owner_l), four_times(rank_l)
    sub = iota((320, 1), 0)
    o_row = jnp.where(sub < 256, sub >> 3, jnp.where(sub < 288, sub - 256, (sub - 288) ^ 18))
    m_row = jnp.where(sub < 256, sub & 7, 8)
    r_row = jnp.where(m_row < 3, 0, jnp.where(m_row < 6, 1, 2))
    c_row = m_row - 3 * r_row
    hit = (owner4 == o_row.astype(F32)) & (rank4 == r_row.astype(F32))
    for tile in range(2):
        q = (iota((1, 128), 1) >> 5) + 4 * tile
        cq = jnp.where(q < 3, q, jnp.where(q < 6, q - 3, -1))
        pick[:, tile * 128:(tile + 1) * 128] = jnp.where(hit & (cq == c_row), 1.0, 0.0).astype(BF16)
    sub96 = iota((96, 1), 0)
    c96 = (sub96 >> 5).astype(F32)
    place = jnp.full((32, 1), -1000.0, F32)
    for k, (dz, dy) in enumerate(NEAR + ((0, 0),)):
        near = moved(8 - dz, 4 - dy)
        place = jnp.where(owner_s == near.astype(F32), float(k * 32), place)
        place = jnp.where(owner_s == antipode(near).astype(F32), float(k * 32 + 16), place)
    target96 = jnp.concatenate([place + within_s] * 3, axis=0) + 5 * c96
    meta_send[...] = jnp.where(lane1 < SLOTS, owner_l * 16 + rank_l * 5 + within_l, 9999.0)
    gather_one[...] = jnp.where(iota((96, 512), 1).astype(F32) == target96, 1.0, 0.0).astype(BF16)
    own_s = (b * 16 + iota((16, 1), 0)).astype(F32)
    place48 = jnp.concatenate([place_s, own_s], axis=0)
    slot_one[...] = jnp.where(iota((48, 128), 1).astype(F32) == place48, 1.0, 0.0).astype(BF16)
    for n, src in enumerate((free, mass)):
        rows = [src[w, 0:1, i * 128:(i + 1) * 128] for i in range(3) for w in range(5)]
        home[0, n] = jnp.concatenate(rows + [jnp.zeros((1, 128), F32)], axis=0)

    con_recv[b] = con_send[...]

    pltpu.make_async_remote_copy(
        src_ref=home.at[0], dst_ref=home.at[1], send_sem=home_s, recv_sem=home_r,
        device_id={"cont": antipode(c)}, device_id_type=MESH,
    ).start()

    def send_meta(p):
        pltpu.make_async_remote_copy(
            src_ref=meta_send, dst_ref=meta_recv.at[c], send_sem=meta_s, recv_sem=meta_r,
            device_id={"cont": p}, device_id_type=MESH,
        ).start()

    over_cont(send_meta)
    meta_recv[c] = meta_send[...]

    drain(tab_recv.at[pl.ds(0, 7)], tab_r)
    imp_a[...] = mm(slot_one[...], tab_recv[:, 0].reshape(128, 128))
    imp_b[...] = mm(slot_one[...], tab_recv[:, 1].reshape(128, 128))
    for cp in blocks:
        cp.wait()

    low32 = lane32 < 64

    def forces():
        ya, yb = imp_a[0:32, :], imp_b[0:32, :]
        turned = half_turn(ya)
        pattern = jnp.concatenate(
            [ya, jnp.where(low32, yb, turned), jnp.where(low32, turned, half_turn(yb))], axis=1
        ).astype(BF16)
        halves = []
        row = iota((16, 768), 0)
        lane = iota((16, 768), 1) // 192
        for h in range(2):
            rep = jnp.concatenate([pattern[16 * h:16 * h + 16]] * 2, axis=1)
            acc = jnp.zeros((16, 384), F32)
            for g in range(0, 16, 4):
                s = 16 * h + g
                n = min(4, SLOTS - s)
                lhs = jnp.where(lane + g == row, rep, jnp.zeros_like(rep))[:, :n * 192]
                acc = acc + mm(lhs, jac[s:s + n].reshape(n * 192, 384))
            halves.append(acc)
        return jnp.concatenate(halves, axis=0)

    def locals_of(v, h):
        row = iota((16, 768), 0) // 2
        lane = iota((16, 768), 1) // 384
        rep = jnp.concatenate([v[16 * h:16 * h + 16]] * 2, axis=1)
        acc = jnp.zeros((16, 384), F32)
        for g in range(0, 8, 2):
            p = 8 * h + g
            n = min(2, SLOTS // 2 - p)
            lhs = jnp.where(lane + g == row, rep, jnp.zeros_like(rep))[:, :n * 384]
            acc = acc + mm(lhs, jact[p:p + n].reshape(n * 384, 384))
        return acc

    def sweep(t, carry):
        sf = forces()
        most = jnp.max(jnp.abs(sf), axis=0, keepdims=True)
        most = jnp.maximum(jnp.maximum(most[:, 0:128], most[:, 128:256]), most[:, 256:384])
        most = jnp.max(most, axis=1, keepdims=True)
        power = jnp.floor(jnp.log2(jnp.maximum(jnp.broadcast_to(most, (1, 128)), 1e-30))) + 1.0
        scale = jnp.exp2(15.0 - power)
        code = jnp.clip(jnp.round(sf * jnp.concatenate([scale] * 3, axis=1)), -32767.0, 32767.0)
        hi, mid = split(code)
        stacked = jnp.concatenate(
            [part[:, n * 128:(n + 1) * 128] for part in (hi, mid) for n in range(3)], axis=0
        )
        packed = mm(pick[:, 0:192], stacked).astype(I32)
        other = jnp.concatenate([packed[8 * (o ^ 18):8 * (o ^ 18) + 8] for o in range(32)], axis=0)
        force_send[t, :, 0:8, :] = (packed[0:256] * 65536 + other).reshape(32, 8, 128)
        force_send[t, :, 8:9, :] = (packed[256:288] * 65536 + packed[288:320]).reshape(32, 1, 128)
        force_send[t, :, 9:10, :] = jnp.broadcast_to(power.astype(I32).reshape(1, 1, 128), (32, 1, 128))

        def send_force(p):
            pltpu.make_async_remote_copy(
                src_ref=force_send.at[t, p], dst_ref=force_recv.at[t, c], send_sem=force_s.at[t],
                recv_sem=force_r.at[t], device_id={"cont": p}, device_id_type=MESH,
            ).start()

        over_cont(send_force)
        force_recv[t, c] = force_send[t, c]

        @pl.when(t == 0)
        def _():
            send_body(con_send, con_recv.at[b], con_s, con_r)
            drain(home.at[1], home_r)
            drain(meta_recv.at[pl.ds(0, 31)], meta_r)
            codes = meta_recv[...].reshape(32, 128)
            line = iota((32, 8, 128), 1)
            lane288 = iota((288, 128), 1).astype(F32)
            sub288 = iota((288, 128), 0)
            m288 = jnp.where(sub288 < 256, sub288 & 7, 8)
            col288 = (m288 - 3 * jnp.where(m288 < 3, 0, jnp.where(m288 < 6, 1, 2))).astype(F32)
            for role, h in enumerate((c, antipode(c))):
                rel = codes - (16 * h).astype(F32)
                found = []
                for r in range(3):
                    fits = (rel >= 5 * r) & (rel < 5 * r + 5)
                    one = jnp.sum(jnp.where(fits, rel - (5 * r - 1), 0.0), axis=1, keepdims=True)
                    found.append(jnp.broadcast_to(one, (32, 128)))
                wide = [jnp.broadcast_to(f.reshape(32, 1, 128), (32, 8, 128)) for f in found]
                rows = jnp.where(line < 3, wide[0], jnp.where(line < 6, wide[1], wide[2])).reshape(256, 128)
                rows = jnp.concatenate([rows, found[2]], axis=0)
                hits = (rows > 0.0) & (lane288 == rows - 1.0 + 5 * col288)
                meta = jnp.concatenate([jnp.where(hits, 1.0, 0.0), jnp.zeros((96, 128), F32)], axis=0)
                owner_one[role] = jnp.transpose(meta)[0:16].astype(BF16)
            for p in range(SLOTS // 2):
                jact[p] = jnp.transpose(jac[2 * p:2 * p + 2].reshape(384, 384))
            drain(con_recv.at[pl.ds(0, 7)], con_r)
            for h in range(2):
                got_ids = con_recv[0, 4, 8 * h:8 * h + 1, :]
                for d in range(1, 8):
                    got_ids = got_ids + con_recv[d, 4, 8 * h:8 * h + 1, :]
                row_one[:, h * 128:(h + 1) * 128] = jnp.where(got_ids == place48, 1.0, 0.0).astype(BF16)
            low48 = iota((48, 128), 1) < 64

            def exact(n):
                plane = con_recv[:, n].reshape(128, 128)
                p0, p1 = split(plane)
                p2 = (plane - p0.astype(F32) - p1.astype(F32)).astype(BF16)
                return mm(slot_one[...], p0) + (mm(slot_one[...], p1) + mm(slot_one[...], p2))

            imp_a[...] = exact(0)
            both = exact(1)
            imp_b[...] = jnp.where(low48, both, 0.0)
            fric48[...] = jnp.where(low48, half_turn(both), both)
            step_a[...] = exact(2)
            both = exact(3)
            step_b[...] = both
            shift48[...] = jnp.where(low48, half_turn(both), 0.0)

        drain(force_recv.at[t, pl.ds(0, 31)], force_r.at[t])
        word = jnp.concatenate(
            [force_recv[t, :, 0:8, :].reshape(256, 128), force_recv[t, :, 8:9, :].reshape(32, 128)], axis=0
        )
        unit = jnp.exp2(force_recv[t, :, 9:10, :].reshape(32, 128).astype(F32) - 15.0)
        units = jnp.concatenate(
            [jnp.broadcast_to(unit.reshape(32, 1, 128), (32, 8, 128)).reshape(256, 128), unit], axis=0
        )
        upper = (word + 32768) >> 16
        both_homes = []
        for role, value in enumerate((upper, word - (upper << 16))):
            parts = jnp.concatenate(split(value.astype(F32) * units), axis=1)
            force = mm(owner_one[role, :, 0:288], parts)
            force = force[:, 0:128] + force[:, 128:256]
            both_homes.append(home[role, 0] + home[role, 1] * force)
        velocity = both_homes[0]

        @pl.when(t == SWEEPS)
        def _():
            for n in range(3):
                for w in range(5):
                    i, p = divmod(w * 3 + n, 5)
                    out[3 + i, 0:1, p * 128:(p + 1) * 128] = velocity[n * 5 + w:n * 5 + w + 1]

        @pl.when(t < SWEEPS)
        def _():
            vel_send[t] = jnp.concatenate(both_homes, axis=0).astype(BF16)
            for k, (dz, dy) in enumerate(NEAR):
                pltpu.make_async_remote_copy(
                    src_ref=vel_send.at[t], dst_ref=vel_recv.at[t, k], send_sem=vel_s.at[t],
                    recv_sem=vel_r.at[t], device_id={"cont": moved(dz, dy)}, device_id_type=MESH,
                ).start()
            vel_recv[t, 15] = vel_send[t]
            drain(vel_recv.at[t, pl.ds(0, 15)], vel_r.at[t])
            vs = mm(gather_one[...], vel_recv[t].reshape(512, 128)).astype(BF16)
            v = jnp.concatenate([vs[0:32], vs[32:64], vs[64:96]], axis=1)
            even = (iota((16, 128), 0) & 1) == 0
            for h in range(2):
                loc = locals_of(v, h)
                l0, l1, l2 = loc[:, 0:128], loc[:, 128:256], loc[:, 256:384]
                t2 = half_turn(l2)
                la = jnp.where(even, l0, jnp.where(low16, half_turn(l1), t2))
                lb = jnp.where(even, l1, t2)
                ahi, amid = split(la)
                bhi = lb.astype(BF16).astype(F32)
                loc_send[t, h, 0] = ahi
                loc_send[t, h, 1] = amid
                loc_send[t, h, 2] = jnp.where(low16, bhi, half_turn(lb - bhi)).astype(BF16)
                send_body(loc_send.at[t, h], loc_recv.at[t, h, b], loc_s.at[t, h], loc_r.at[t, h])
                loc_recv[t, h, b] = loc_send[t, h]
            lv = jnp.zeros((48, 384), F32)
            for h in range(2):
                drain(loc_recv.at[t, h, pl.ds(0, 7)], loc_r.at[t, h])
                got_loc = jnp.concatenate([loc_recv[t, h, :, n].reshape(128, 128) for n in range(3)], axis=1)
                lv = lv + mm(row_one[:, h * 128:(h + 1) * 128], got_loc)
            lva = lv[:, 0:128] + lv[:, 128:256]
            lvb = lv[:, 256:384] + half_turn(lv[:, 256:384])
            low = iota((48, 128), 1) < 64
            fr = fric48[...]
            ta = imp_a[...] - step_a[...] * (lva + shift48[...])
            tb = imp_b[...] - step_b[...] * lvb
            normal = jnp.where(low, jnp.maximum(ta, 0.0), 0.0)
            lim_a = fr * half_turn(normal)
            lim_b = fr * normal
            live = fr >= 0.0
            new_a = jnp.where(low, normal, jnp.clip(ta, -lim_a, lim_a))
            imp_a[...] = jnp.where(live, new_a, 0.0)
            imp_b[...] = jnp.where(live & low, jnp.clip(tb, -lim_b, lim_b), 0.0)

        return carry

    lax.fori_loop(0, SWEEPS + 1, sweep, 0)

    own_a, own_b = imp_a[32:48, :], imp_b[32:48, :]
    ae, ao, be, bo = own_a[0:8], own_a[8:16], own_b[0:8], own_b[8:16]
    outs = (
        jnp.where(low8, ae, half_turn(ao)),
        jnp.where(low8, half_turn(ae), ao),
        jnp.where(low8, be, half_turn(bo)),
    )
    for i in range(3):
        for p in range(5):
            out[i, 0:1, p * 128:(p + 1) * 128] = outs[i][p:p + 1]

    drain(tab_recv.at[pl.ds(0, 7)], tab_s)
    drain(con_recv.at[pl.ds(0, 7)], con_s)
    drain(meta_recv.at[pl.ds(0, 31)], meta_s)
    drain(home.at[1], home_s)
    for t in range(SWEEPS + 1):
        drain(force_recv.at[t, pl.ds(0, 31)], force_s.at[t])
        if t < SWEEPS:
            drain(vel_recv.at[t, pl.ds(0, 15)], vel_s.at[t])
            for h in range(2):
                drain(loc_recv.at[t, h, pl.ds(0, 7)], loc_s.at[t, h])


def shards(jacobian, row, col, live, warm, step, bias, fric, free, mass):
    dma = pltpu.SemaphoreType.DMA
    passes = SWEEPS + 1
    hbm = pl.BlockSpec(memory_space=pl.ANY)
    vmem = pl.BlockSpec(memory_space=pltpu.VMEM)
    out = pl.pallas_call(
        kernel,
        out_shape=jax.ShapeDtypeStruct((6, 1, 640), F32),
        in_specs=[hbm] * 10,
        out_specs=vmem,
        scratch_shapes=[
            pltpu.VMEM((SLOTS, 3, 64, 384), BF16),
            pltpu.VMEM((1, SLOTS), I32),
            pltpu.VMEM((1, SLOTS), I32),
            pltpu.VMEM((1, 10), I32),
            pltpu.VMEM((3, 1, 640), F32),
            pltpu.VMEM((3, 1, 640), F32),
            pltpu.VMEM((1, 640), F32),
            pltpu.VMEM((1, 640), F32),
            pltpu.VMEM((5, 1, 384), F32),
            pltpu.VMEM((5, 1, 384), F32),
            pltpu.VMEM((SLOTS // 2, 384, 384), BF16),
            pltpu.VMEM((8, 128), I32),
            pltpu.VMEM((320, 256), BF16),
            pltpu.VMEM((2, 16, 384), BF16),
            pltpu.VMEM((48, 128), BF16),
            pltpu.VMEM((48, 256), BF16),
            pltpu.VMEM((96, 512), BF16),
            pltpu.VMEM((48, 128), F32),
            pltpu.VMEM((48, 128), F32),
            pltpu.VMEM((48, 128), F32),
            pltpu.VMEM((48, 128), F32),
            pltpu.VMEM((48, 128), F32),
            pltpu.VMEM((48, 128), F32),
            pltpu.VMEM((2, 2, 16, 128), F32),
            pltpu.VMEM((2, 16, 128), BF16),
            pltpu.VMEM((8, 2, 16, 128), BF16),
            pltpu.VMEM((5, 16, 128), F32),
            pltpu.VMEM((8, 5, 16, 128), F32),
            pltpu.VMEM((1, 128), F32),
            pltpu.VMEM((32, 1, 128), F32),
            pltpu.VMEM((passes, 32, 10, 128), I32),
            pltpu.VMEM((passes, 32, 10, 128), I32),
            pltpu.VMEM((SWEEPS, 32, 128), BF16),
            pltpu.VMEM((SWEEPS, 16, 32, 128), BF16),
            pltpu.VMEM((SWEEPS, 2, 3, 16, 128), BF16),
            pltpu.VMEM((SWEEPS, 2, 8, 3, 16, 128), BF16),
            dma((5,)), dma((9,)), dma, dma, dma, dma, dma, dma, dma, dma,
            dma((passes,)), dma((passes,)), dma((SWEEPS,)), dma((SWEEPS,)), dma((SWEEPS, 2)), dma((SWEEPS, 2)),
        ],
        compiler_params=pltpu.CompilerParams(
            collective_id=0, has_side_effects=True, vmem_limit_bytes=63 << 20
        ),
        name="sweeps",
    )(jacobian.reshape(jacobian.shape[1:]), row, col, live, warm, step, bias, fric,
      free.transpose(1, 0, 2), mass.transpose(1, 0, 2))
    return out[0:3], out[3:6].reshape(5, 1, 384).transpose(1, 0, 2)


def solution(mesh):
    placed = (
        P("body", "cont", None, None, None),
        P("body", "cont"),
        P("body", "cont"),
        P("cont", "body"),
        P(None, "cont", "body"),
        P(None, "cont", "body"),
        P("cont", "body"),
        P("cont", "body"),
        P("body", "cont", None),
        P("body", "cont", None),
    )
    return jax.shard_map(
        shards,
        mesh=mesh,
        in_specs=placed,
        out_specs=(P(None, "cont", "body"), P("body", "cont", None)),
        check_vma=False,
    )
```

```python
import jax
import jax.numpy as jnp
from jax import lax
from jax.experimental import pallas as pl
from jax.experimental.pallas import tpu as pltpu
from jax.sharding import PartitionSpec as P

MESH = pl.DeviceIdType.MESH
SWEEPS = 3
SLOTS = 30
NEAR = (
    (1, 2), (7, 2), (2, 1), (6, 1), (2, 0), (6, 0), (1, 1), (1, 3), (7, 1), (7, 3), (0, 2),
    (1, 0), (7, 0), (0, 1), (0, 3),
)
F32, BF16, I32 = jnp.float32, jnp.bfloat16, jnp.int32


def iota(shape, dim):
    return lax.broadcasted_iota(I32, shape, dim)


def half_turn(x):
    return pltpu.roll(x, 64, axis=x.ndim - 1)


def split(x):
    hi = x.astype(BF16)
    mid = (x - hi.astype(F32)).astype(BF16)
    return hi, mid


def mm(a, b):
    return jnp.dot(a, b, preferred_element_type=F32)


def kernel(
    jac_in, row_in, col_in, live_in, warm_in, step_in, bias_in, fric_in, free_in, mass_in,
    out,
    jac, rowv, colv, livev, warm, step, bias, fric, free, mass,
    jact, ids, pick, owner_one, slot_one, row_one, gather_one,
    imp_a, imp_b, step_a, step_b, fric48, shift48, home,
    tab_send, tab_recv, con_send, con_recv, meta_send, meta_recv,
    force_send, force_recv, vel_send, vel_recv, loc_send, loc_recv,
    jac_sem, in_sem, home_s, home_r, tab_s, tab_r, con_s, con_r, meta_s, meta_r,
    force_s, force_r, vel_s, vel_r, loc_s, loc_r,
):
    b, c = lax.axis_index("body"), lax.axis_index("cont")
    x, core, z, y = b // 2, b % 2, c // 4, c % 4

    def cont_peer(k):
        i, j = k // 4, k % 4
        dz = 4 + (1 - 2 * (i % 2)) * ((i + 1) // 2)
        dy = 2 + (1 - 2 * (j % 2)) * ((j + 1) // 2)
        return ((z + dz) % 8) * 4 + (y + dy) % 4

    def moved(dz, dy):
        return ((z + dz) % 8) * 4 + (y + dy) % 4

    def antipode(p):
        return ((p // 4 + 4) % 8) * 4 + (p % 4 + 2) % 4

    body_peers = [
        ((x + dx) % 4) * 2 + (core + dc) % 2
        for dx, dc in ((2, 1), (2, 0), (1, 1), (3, 1), (1, 0), (3, 0), (0, 1))
    ]

    def over_cont(go):
        def one(k, carry):
            go(cont_peer(k))
            return carry

        lax.fori_loop(0, 31, one, 0)

    def send_body(src, dst, ssem, rsem):
        for p in body_peers:
            pltpu.make_async_remote_copy(
                src_ref=src, dst_ref=dst, send_sem=ssem, recv_sem=rsem,
                device_id={"body": p}, device_id_type=MESH,
            ).start()

    def drain(ref, sem):
        pltpu.make_async_copy(ref, ref, sem).wait()

    bar = pltpu.get_barrier_semaphore()
    over_cont(lambda p: pl.semaphore_signal(bar, inc=1, device_id={"cont": p}, device_id_type=MESH))
    for p in body_peers:
        pl.semaphore_signal(bar, inc=1, device_id={"body": p}, device_id_type=MESH)

    pairs = (
        (warm_in, warm), (live_in, livev), (row_in, rowv), (col_in, colv), (step_in, step),
        (bias_in, bias), (fric_in, fric), (free_in, free), (mass_in, mass),
    )
    small = [pltpu.make_async_copy(s, d, in_sem.at[n]) for n, (s, d) in enumerate(pairs)]
    for cp in small:
        cp.start()
    blocks = [
        pltpu.make_async_copy(jac_in.at[pl.ds(n * 6, 6)], jac.at[pl.ds(n * 6, 6)], jac_sem.at[n])
        for n in range(5)
    ]
    for cp in blocks:
        cp.start()
    for cp in small[:2]:
        cp.wait()

    lane16 = iota((16, 128), 1)
    low16 = lane16 < 64
    lane8 = iota((8, 128), 1)
    low8 = lane8 < 64

    def rows_of(get):
        parts = [get(p).astype(F32) for p in range(5)]
        return jnp.concatenate(parts + [jnp.zeros((3, 128), F32)], axis=0)

    def planes(ref):
        w0, w1, w2 = [rows_of(lambda p, i=i: ref[i, 0:1, p * 128:(p + 1) * 128]) for i in range(3)]
        even = jnp.where(low8, w0, half_turn(w1))
        odd = jnp.where(low8, half_turn(w0), w1)
        return jnp.concatenate([even, odd], 0), jnp.concatenate([w2, half_turn(w2)], 0)

    def high_plane(ref):
        f = rows_of(lambda p: ref[0:1, p * 128:(p + 1) * 128])
        return jnp.concatenate([half_turn(f), f], 0)

    sub10 = iota((16, 10), 0)
    block_of_row = 2 * (sub10 & 7) + (sub10 >> 3)
    live_row = jnp.sum(
        jnp.where(iota((16, 10), 1) == block_of_row, livev[...].astype(F32), 0.0), axis=1, keepdims=True
    )
    active = (lane16 & 63).astype(F32) < live_row
    wa, wb = planes(warm)
    wa, wb = jnp.where(active, wa, 0.0), jnp.where(active & low16, wb, 0.0)
    tab_send[0] = wa.astype(BF16)
    tab_send[1] = wb.astype(BF16)
    pl.semaphore_wait(bar, 38)
    send_body(tab_send, tab_recv.at[b], tab_s, tab_r)
    tab_recv[b] = tab_send[...]

    for cp in small[2:]:
        cp.wait()
    sa, sb = planes(step)
    con_send[0] = wa
    con_send[1] = jnp.where(low16, wb, jnp.where(active, high_plane(fric), -1.0))
    con_send[2] = sa
    con_send[3] = jnp.where(low16, sb, high_plane(bias))

    ids[0:1, :] = jnp.where(iota((1, 128), 1) < 32, 9999, 0)
    ids[1:2, :] = jnp.where(iota((1, 128), 1) < 32, 10000, 0)
    ids[0:1, 0:SLOTS] = rowv[...]
    ids[1:2, 0:SLOTS] = colv[...]
    lane1 = iota((1, 128), 1)
    row_l = ids[0:1, :]
    dev = (row_l * 52429) >> 19
    kk = row_l - 10 * dev
    place_l = jnp.where(
        lane1 < SLOTS, dev * 16 + (kk & 1) * 8 + (kk >> 1), jnp.where(lane1 < 32, 9999, 0)
    ).astype(F32)
    col_l = ids[1:2, :]
    owner_i = (col_l * 52429) >> 18
    within_l = (col_l - 5 * owner_i).astype(F32)
    owner_l = owner_i.astype(F32)

    sub32, lane32 = iota((32, 128), 0), iota((32, 128), 1)

    def down(v):
        return jnp.sum(jnp.where(sub32 == lane32, jnp.broadcast_to(v, (32, 128)), 0.0), axis=1, keepdims=True)

    place_s, owner_s, within_s = down(place_l), down(owner_l), down(within_l)
    rank_l = jnp.sum(
        jnp.where((owner_s == owner_l) & (sub32 < lane32) & (lane32 < 32), 1.0, 0.0), axis=0, keepdims=True
    )
    place8 = jnp.broadcast_to(place_l, (8, 128))
    con_send[4, 0:8, :] = pltpu.roll(jnp.where(lane8 < 16, place8, 0.0), b * 16, axis=1)
    con_send[4, 8:16, :] = pltpu.roll(jnp.where((lane8 >= 16) & (lane8 < 32), place8, 0.0), (b * 16 + 112) % 128, axis=1)

    def four_times(v):
        v = jnp.broadcast_to(v, (8, 128))
        v = v + pltpu.roll(v, 32, axis=1)
        return (v + pltpu.roll(v, 64, axis=1))[0:1]

    owner4, rank4 = four_times(owner_l), four_times(rank_l)
    sub = iota((320, 1), 0)
    o_row = jnp.where(sub < 256, sub >> 3, jnp.where(sub < 288, sub - 256, (sub - 288) ^ 18))
    m_row = jnp.where(sub < 256, sub & 7, 8)
    r_row = jnp.where(m_row < 3, 0, jnp.where(m_row < 6, 1, 2))
    c_row = m_row - 3 * r_row
    hit = (owner4 == o_row.astype(F32)) & (rank4 == r_row.astype(F32))
    for tile in range(2):
        q = (iota((1, 128), 1) >> 5) + 4 * tile
        cq = jnp.where(q < 3, q, jnp.where(q < 6, q - 3, -1))
        pick[:, tile * 128:(tile + 1) * 128] = jnp.where(hit & (cq == c_row), 1.0, 0.0).astype(BF16)
    sub96 = iota((96, 1), 0)
    c96 = (sub96 >> 5).astype(F32)
    place = jnp.full((32, 1), -1000.0, F32)
    for k, (dz, dy) in enumerate(NEAR + ((0, 0),)):
        near = moved(8 - dz, 4 - dy)
        place = jnp.where(owner_s == near.astype(F32), float(k * 32), place)
        place = jnp.where(owner_s == antipode(near).astype(F32), float(k * 32 + 16), place)
    target96 = jnp.concatenate([place + within_s] * 3, axis=0) + 5 * c96
    meta_send[...] = jnp.where(lane1 < SLOTS, owner_l * 16 + rank_l * 5 + within_l, 9999.0)
    gather_one[...] = jnp.where(iota((96, 512), 1).astype(F32) == target96, 1.0, 0.0).astype(BF16)
    own_s = (b * 16 + iota((16, 1), 0)).astype(F32)
    place48 = jnp.concatenate([place_s, own_s], axis=0)
    slot_one[...] = jnp.where(iota((48, 128), 1).astype(F32) == place48, 1.0, 0.0).astype(BF16)
    for n, src in enumerate((free, mass)):
        rows = [src[w, 0:1, i * 128:(i + 1) * 128] for i in range(3) for w in range(5)]
        home[0, n] = jnp.concatenate(rows + [jnp.zeros((1, 128), F32)], axis=0)

    con_recv[b] = con_send[...]

    pltpu.make_async_remote_copy(
        src_ref=home.at[0], dst_ref=home.at[1], send_sem=home_s, recv_sem=home_r,
        device_id={"cont": antipode(c)}, device_id_type=MESH,
    ).start()

    def send_meta(p):
        pltpu.make_async_remote_copy(
            src_ref=meta_send, dst_ref=meta_recv.at[c], send_sem=meta_s, recv_sem=meta_r,
            device_id={"cont": p}, device_id_type=MESH,
        ).start()

    over_cont(send_meta)
    meta_recv[c] = meta_send[...]

    drain(tab_recv.at[pl.ds(0, 7)], tab_r)
    imp_a[...] = mm(slot_one[...], tab_recv[:, 0].reshape(128, 128))
    imp_b[...] = mm(slot_one[...], tab_recv[:, 1].reshape(128, 128))
    for cp in blocks:
        cp.wait()

    low32 = lane32 < 64

    def forces():
        ya, yb = imp_a[0:32, :], imp_b[0:32, :]
        turned = half_turn(ya)
        pattern = jnp.concatenate(
            [ya, jnp.where(low32, yb, turned), jnp.where(low32, turned, half_turn(yb))], axis=1
        ).astype(BF16)
        halves = []
        row = iota((16, 768), 0)
        lane = iota((16, 768), 1) // 192
        for h in range(2):
            rep = jnp.concatenate([pattern[16 * h:16 * h + 16]] * 2, axis=1)
            acc = jnp.zeros((16, 384), F32)
            for g in range(0, 16, 4):
                s = 16 * h + g
                n = min(4, SLOTS - s)
                lhs = jnp.where(lane + g == row, rep, jnp.zeros_like(rep))[:, :n * 192]
                acc = acc + mm(lhs, jac[s:s + n].reshape(n * 192, 384))
            halves.append(acc)
        return jnp.concatenate(halves, axis=0)

    def locals_of(v, h):
        row = iota((16, 768), 0) // 2
        lane = iota((16, 768), 1) // 384
        rep = jnp.concatenate([v[16 * h:16 * h + 16]] * 2, axis=1)
        acc = jnp.zeros((16, 384), F32)
        for g in range(0, 8, 2):
            p = 8 * h + g
            n = min(2, SLOTS // 2 - p)
            lhs = jnp.where(lane + g == row, rep, jnp.zeros_like(rep))[:, :n * 384]
            acc = acc + mm(lhs, jact[p:p + n].reshape(n * 384, 384))
        return acc

    def sweep(t, carry):
        sf = forces()
        most = jnp.max(jnp.abs(sf), axis=0, keepdims=True)
        most = jnp.maximum(jnp.maximum(most[:, 0:128], most[:, 128:256]), most[:, 256:384])
        most = jnp.max(most, axis=1, keepdims=True)
        power = jnp.floor(jnp.log2(jnp.maximum(jnp.broadcast_to(most, (1, 128)), 1e-30))) + 1.0
        scale = jnp.exp2(15.0 - power)
        code = jnp.clip(jnp.round(sf * jnp.concatenate([scale] * 3, axis=1)), -32767.0, 32767.0)
        hi, mid = split(code)
        stacked = jnp.concatenate(
            [part[:, n * 128:(n + 1) * 128] for part in (hi, mid) for n in range(3)], axis=0
        )
        packed = mm(pick[:, 0:192], stacked).astype(I32)
        other = jnp.concatenate([packed[8 * (o ^ 18):8 * (o ^ 18) + 8] for o in range(32)], axis=0)
        force_send[t, :, 0:8, :] = (packed[0:256] * 65536 + other).reshape(32, 8, 128)
        force_send[t, :, 8:9, :] = (packed[256:288] * 65536 + packed[288:320]).reshape(32, 1, 128)
        force_send[t, :, 9:10, :] = jnp.broadcast_to(power.astype(I32).reshape(1, 1, 128), (32, 1, 128))

        def send_force(p):
            pltpu.make_async_remote_copy(
                src_ref=force_send.at[t, p], dst_ref=force_recv.at[t, c], send_sem=force_s.at[t],
                recv_sem=force_r.at[t], device_id={"cont": p}, device_id_type=MESH,
            ).start()

        over_cont(send_force)
        force_recv[t, c] = force_send[t, c]

        @pl.when(t == 0)
        def _():
            send_body(con_send, con_recv.at[b], con_s, con_r)
            drain(home.at[1], home_r)
            drain(meta_recv.at[pl.ds(0, 31)], meta_r)
            codes = meta_recv[...].reshape(32, 128)
            line = iota((32, 8, 128), 1)
            lane288 = iota((288, 128), 1).astype(F32)
            sub288 = iota((288, 128), 0)
            m288 = jnp.where(sub288 < 256, sub288 & 7, 8)
            col288 = (m288 - 3 * jnp.where(m288 < 3, 0, jnp.where(m288 < 6, 1, 2))).astype(F32)
            for role, h in enumerate((c, antipode(c))):
                rel = codes - (16 * h).astype(F32)
                found = []
                for r in range(3):
                    fits = (rel >= 5 * r) & (rel < 5 * r + 5)
                    one = jnp.sum(jnp.where(fits, rel - (5 * r - 1), 0.0), axis=1, keepdims=True)
                    found.append(jnp.broadcast_to(one, (32, 128)))
                wide = [jnp.broadcast_to(f.reshape(32, 1, 128), (32, 8, 128)) for f in found]
                rows = jnp.where(line < 3, wide[0], jnp.where(line < 6, wide[1], wide[2])).reshape(256, 128)
                rows = jnp.concatenate([rows, found[2]], axis=0)
                hits = (rows > 0.0) & (lane288 == rows - 1.0 + 5 * col288)
                meta = jnp.concatenate([jnp.where(hits, 1.0, 0.0), jnp.zeros((96, 128), F32)], axis=0)
                owner_one[role] = jnp.transpose(meta)[0:16].astype(BF16)
            for p in range(SLOTS // 2):
                jact[p] = jnp.transpose(jac[2 * p:2 * p + 2].reshape(384, 384))
            drain(con_recv.at[pl.ds(0, 7)], con_r)
            for h in range(2):
                got_ids = con_recv[0, 4, 8 * h:8 * h + 1, :]
                for d in range(1, 8):
                    got_ids = got_ids + con_recv[d, 4, 8 * h:8 * h + 1, :]
                row_one[:, h * 128:(h + 1) * 128] = jnp.where(got_ids == place48, 1.0, 0.0).astype(BF16)
            low48 = iota((48, 128), 1) < 64

            def exact(n):
                plane = con_recv[:, n].reshape(128, 128)
                p0, p1 = split(plane)
                p2 = (plane - p0.astype(F32) - p1.astype(F32)).astype(BF16)
                return mm(slot_one[...], p0) + (mm(slot_one[...], p1) + mm(slot_one[...], p2))

            imp_a[...] = exact(0)
            both = exact(1)
            imp_b[...] = jnp.where(low48, both, 0.0)
            fric48[...] = jnp.where(low48, half_turn(both), both)
            step_a[...] = exact(2)
            both = exact(3)
            step_b[...] = both
            shift48[...] = jnp.where(low48, half_turn(both), 0.0)

        drain(force_recv.at[t, pl.ds(0, 31)], force_r.at[t])
        word = jnp.concatenate(
            [force_recv[t, :, 0:8, :].reshape(256, 128), force_recv[t, :, 8:9, :].reshape(32, 128)], axis=0
        )
        unit = jnp.exp2(force_recv[t, :, 9:10, :].reshape(32, 128).astype(F32) - 15.0)
        units = jnp.concatenate(
            [jnp.broadcast_to(unit.reshape(32, 1, 128), (32, 8, 128)).reshape(256, 128), unit], axis=0
        )
        upper = (word + 32768) >> 16
        both_homes = []
        for role, value in enumerate((upper, word - (upper << 16))):
            parts = jnp.concatenate(split(value.astype(F32) * units), axis=1)
            force = mm(owner_one[role, :, 0:288], parts)
            force = force[:, 0:128] + force[:, 128:256]
            both_homes.append(home[role, 0] + home[role, 1] * force)
        velocity = both_homes[0]

        @pl.when(t == SWEEPS)
        def _():
            for n in range(3):
                for w in range(5):
                    i, p = divmod(w * 3 + n, 5)
                    out[3 + i, 0:1, p * 128:(p + 1) * 128] = velocity[n * 5 + w:n * 5 + w + 1]

        @pl.when(t < SWEEPS)
        def _():
            vel_send[t] = jnp.concatenate(both_homes, axis=0).astype(BF16)
            for k, (dz, dy) in enumerate(NEAR):
                pltpu.make_async_remote_copy(
                    src_ref=vel_send.at[t], dst_ref=vel_recv.at[t, k], send_sem=vel_s.at[t],
                    recv_sem=vel_r.at[t], device_id={"cont": moved(dz, dy)}, device_id_type=MESH,
                ).start()
            vel_recv[t, 15] = vel_send[t]
            drain(vel_recv.at[t, pl.ds(0, 15)], vel_r.at[t])
            vs = mm(gather_one[...], vel_recv[t].reshape(512, 128)).astype(BF16)
            v = jnp.concatenate([vs[0:32], vs[32:64], vs[64:96]], axis=1)
            even = (iota((16, 128), 0) & 1) == 0
            for h in range(2):
                loc = locals_of(v, h)
                l0, l1, l2 = loc[:, 0:128], loc[:, 128:256], loc[:, 256:384]
                t2 = half_turn(l2)
                la = jnp.where(even, l0, jnp.where(low16, half_turn(l1), t2))
                lb = jnp.where(even, l1, t2)
                ahi, amid = split(la)
                bhi = lb.astype(BF16).astype(F32)
                loc_send[t, h, 0] = ahi
                loc_send[t, h, 1] = amid
                loc_send[t, h, 2] = jnp.where(low16, bhi, half_turn(lb - bhi)).astype(BF16)
                send_body(loc_send.at[t, h], loc_recv.at[t, h, b], loc_s.at[t, h], loc_r.at[t, h])
                loc_recv[t, h, b] = loc_send[t, h]
            lv = jnp.zeros((48, 384), F32)
            for h in range(2):
                drain(loc_recv.at[t, h, pl.ds(0, 7)], loc_r.at[t, h])
                got_loc = jnp.concatenate([loc_recv[t, h, :, n].reshape(128, 128) for n in range(3)], axis=1)
                lv = lv + mm(row_one[:, h * 128:(h + 1) * 128], got_loc)
            lva = lv[:, 0:128] + lv[:, 128:256]
            lvb = lv[:, 256:384] + half_turn(lv[:, 256:384])
            low = iota((48, 128), 1) < 64
            fr = fric48[...]
            ta = imp_a[...] - step_a[...] * (lva + shift48[...])
            tb = imp_b[...] - step_b[...] * lvb
            normal = jnp.where(low, jnp.maximum(ta, 0.0), 0.0)
            lim_a = fr * half_turn(normal)
            lim_b = fr * normal
            live = fr >= 0.0
            new_a = jnp.where(low, normal, jnp.clip(ta, -lim_a, lim_a))
            imp_a[...] = jnp.where(live, new_a, 0.0)
            imp_b[...] = jnp.where(live & low, jnp.clip(tb, -lim_b, lim_b), 0.0)

        return carry

    lax.fori_loop(0, SWEEPS + 1, sweep, 0)

    own_a, own_b = imp_a[32:48, :], imp_b[32:48, :]
    ae, ao, be, bo = own_a[0:8], own_a[8:16], own_b[0:8], own_b[8:16]
    outs = (
        jnp.where(low8, ae, half_turn(ao)),
        jnp.where(low8, half_turn(ae), ao),
        jnp.where(low8, be, half_turn(bo)),
    )
    for i in range(3):
        for p in range(5):
            out[i, 0:1, p * 128:(p + 1) * 128] = outs[i][p:p + 1]

    drain(tab_recv.at[pl.ds(0, 7)], tab_s)
    drain(con_recv.at[pl.ds(0, 7)], con_s)
    drain(meta_recv.at[pl.ds(0, 31)], meta_s)
    drain(home.at[1], home_s)
    for t in range(SWEEPS + 1):
        drain(force_recv.at[t, pl.ds(0, 31)], force_s.at[t])
        if t < SWEEPS:
            drain(vel_recv.at[t, pl.ds(0, 15)], vel_s.at[t])
            for h in range(2):
                drain(loc_recv.at[t, h, pl.ds(0, 7)], loc_s.at[t, h])


def shards(jacobian, row, col, live, warm, step, bias, fric, free, mass):
    dma = pltpu.SemaphoreType.DMA
    passes = SWEEPS + 1
    hbm = pl.BlockSpec(memory_space=pl.ANY)
    vmem = pl.BlockSpec(memory_space=pltpu.VMEM)
    out = pl.pallas_call(
        kernel,
        out_shape=jax.ShapeDtypeStruct((6, 1, 640), F32),
        in_specs=[hbm] * 10,
        out_specs=vmem,
        scratch_shapes=[
            pltpu.VMEM((SLOTS, 3, 64, 384), BF16),
            pltpu.VMEM((1, SLOTS), I32),
            pltpu.VMEM((1, SLOTS), I32),
            pltpu.VMEM((1, 10), I32),
            pltpu.VMEM((3, 1, 640), F32),
            pltpu.VMEM((3, 1, 640), F32),
            pltpu.VMEM((1, 640), F32),
            pltpu.VMEM((1, 640), F32),
            pltpu.VMEM((5, 1, 384), F32),
            pltpu.VMEM((5, 1, 384), F32),
            pltpu.VMEM((SLOTS // 2, 384, 384), BF16),
            pltpu.VMEM((8, 128), I32),
            pltpu.VMEM((320, 256), BF16),
            pltpu.VMEM((2, 16, 384), BF16),
            pltpu.VMEM((48, 128), BF16),
            pltpu.VMEM((48, 256), BF16),
            pltpu.VMEM((96, 512), BF16),
            pltpu.VMEM((48, 128), F32),
            pltpu.VMEM((48, 128), F32),
            pltpu.VMEM((48, 128), F32),
            pltpu.VMEM((48, 128), F32),
            pltpu.VMEM((48, 128), F32),
            pltpu.VMEM((48, 128), F32),
            pltpu.VMEM((2, 2, 16, 128), F32),
            pltpu.VMEM((2, 16, 128), BF16),
            pltpu.VMEM((8, 2, 16, 128), BF16),
            pltpu.VMEM((5, 16, 128), F32),
            pltpu.VMEM((8, 5, 16, 128), F32),
            pltpu.VMEM((1, 128), F32),
            pltpu.VMEM((32, 1, 128), F32),
            pltpu.VMEM((passes, 32, 10, 128), I32),
            pltpu.VMEM((passes, 32, 10, 128), I32),
            pltpu.VMEM((SWEEPS, 32, 128), BF16),
            pltpu.VMEM((SWEEPS, 16, 32, 128), BF16),
            pltpu.VMEM((SWEEPS, 2, 3, 16, 128), BF16),
            pltpu.VMEM((SWEEPS, 2, 8, 3, 16, 128), BF16),
            dma((5,)), dma((9,)), dma, dma, dma, dma, dma, dma, dma, dma,
            dma((passes,)), dma((passes,)), dma((SWEEPS,)), dma((SWEEPS,)), dma((SWEEPS, 2)), dma((SWEEPS, 2)),
        ],
        compiler_params=pltpu.CompilerParams(
            collective_id=0, has_side_effects=True, vmem_limit_bytes=32 << 20
        ),
        name="sweeps",
    )(*[
        pltpu.with_memory_space_constraint(v, pltpu.HBM)
        for v in (
            jacobian.reshape(jacobian.shape[1:]), row, col, live, warm, step, bias, fric,
            free.transpose(1, 0, 2), mass.transpose(1, 0, 2),
        )
    ])
    return out[0:3], out[3:6].reshape(5, 1, 384).transpose(1, 0, 2)


def solution(mesh):
    placed = (
        P("body", "cont", None, None, None),
        P("body", "cont"),
        P("body", "cont"),
        P("cont", "body"),
        P(None, "cont", "body"),
        P(None, "cont", "body"),
        P("cont", "body"),
        P("cont", "body"),
        P("body", "cont", None),
        P("body", "cont", None),
    )
    return jax.shard_map(
        shards,
        mesh=mesh,
        in_specs=placed,
        out_specs=(P(None, "cont", "body"), P("body", "cont", None)),
        check_vma=False,
    )
```

```python
import jax
import jax.numpy as jnp
from jax import lax
from jax.experimental import pallas as pl
from jax.experimental.pallas import tpu as pltpu
from jax.sharding import PartitionSpec as P

MESH = pl.DeviceIdType.MESH
SWEEPS = 3
SLOTS = 30
NEAR = (
    (1, 2), (7, 2), (2, 1), (6, 1), (2, 0), (6, 0), (1, 1), (1, 3), (7, 1), (7, 3), (0, 2),
    (1, 0), (7, 0), (0, 1), (0, 3),
)
F32, BF16, I32 = jnp.float32, jnp.bfloat16, jnp.int32


def iota(shape, dim):
    return lax.broadcasted_iota(I32, shape, dim)


def half_turn(x):
    return pltpu.roll(x, 64, axis=x.ndim - 1)


def split(x):
    hi = x.astype(BF16)
    mid = (x - hi.astype(F32)).astype(BF16)
    return hi, mid


def mm(a, b):
    return jnp.dot(a, b, preferred_element_type=F32)


def kernel(
    jac_in, row_in, col_in, live_in, warm_in, step_in, bias_in, fric_in, free_in, mass_in,
    out,
    jac, rowv, colv, livev, warm, step, bias, fric, free, mass,
    jact, ids, pick, owner_one, slot_one, row_one, gather_one,
    imp_a, imp_b, step_a, step_b, fric48, shift48, home,
    tab_send, tab_recv, con_send, con_recv, meta_send, meta_recv,
    force_send, force_recv, vel_send, vel_recv, loc_send, loc_recv,
    jac_sem, in_sem, home_s, home_r, tab_s, tab_r, con_s, con_r, meta_s, meta_r,
    force_s, force_r, vel_s, vel_r, loc_s, loc_r,
):
    b, c = lax.axis_index("body"), lax.axis_index("cont")
    x, core, z, y = b // 2, b % 2, c // 4, c % 4

    def cont_peer(k):
        i, j = k // 4, k % 4
        dz = 4 + (1 - 2 * (i % 2)) * ((i + 1) // 2)
        dy = 2 + (1 - 2 * (j % 2)) * ((j + 1) // 2)
        return ((z + dz) % 8) * 4 + (y + dy) % 4

    def moved(dz, dy):
        return ((z + dz) % 8) * 4 + (y + dy) % 4

    def antipode(p):
        return ((p // 4 + 4) % 8) * 4 + (p % 4 + 2) % 4

    body_peers = [
        ((x + dx) % 4) * 2 + (core + dc) % 2
        for dx, dc in ((2, 1), (2, 0), (1, 1), (3, 1), (1, 0), (3, 0), (0, 1))
    ]

    def over_cont(go):
        for k in range(31):
            go(cont_peer(k))

    def send_body(src, dst, ssem, rsem):
        for p in body_peers:
            pltpu.make_async_remote_copy(
                src_ref=src, dst_ref=dst, send_sem=ssem, recv_sem=rsem,
                device_id={"body": p}, device_id_type=MESH,
            ).start()

    def drain(ref, sem):
        pltpu.make_async_copy(ref, ref, sem).wait()

    bar = pltpu.get_barrier_semaphore()
    over_cont(lambda p: pl.semaphore_signal(bar, inc=1, device_id={"cont": p}, device_id_type=MESH))
    for p in body_peers:
        pl.semaphore_signal(bar, inc=1, device_id={"body": p}, device_id_type=MESH)

    pairs = (
        (warm_in, warm), (live_in, livev), (row_in, rowv), (col_in, colv), (step_in, step),
        (bias_in, bias), (fric_in, fric), (free_in, free), (mass_in, mass),
    )
    small = [pltpu.make_async_copy(s, d, in_sem.at[n]) for n, (s, d) in enumerate(pairs)]
    for cp in small:
        cp.start()
    blocks = [
        pltpu.make_async_copy(jac_in.at[pl.ds(n * 6, 6)], jac.at[pl.ds(n * 6, 6)], jac_sem.at[n])
        for n in range(5)
    ]
    for cp in blocks:
        cp.start()
    for cp in small[:2]:
        cp.wait()

    lane16 = iota((16, 128), 1)
    low16 = lane16 < 64
    lane8 = iota((8, 128), 1)
    low8 = lane8 < 64

    def rows_of(get):
        parts = [get(p).astype(F32) for p in range(5)]
        return jnp.concatenate(parts + [jnp.zeros((3, 128), F32)], axis=0)

    def planes(ref):
        w0, w1, w2 = [rows_of(lambda p, i=i: ref[i, 0:1, p * 128:(p + 1) * 128]) for i in range(3)]
        even = jnp.where(low8, w0, half_turn(w1))
        odd = jnp.where(low8, half_turn(w0), w1)
        return jnp.concatenate([even, odd], 0), jnp.concatenate([w2, half_turn(w2)], 0)

    def high_plane(ref):
        f = rows_of(lambda p: ref[0:1, p * 128:(p + 1) * 128])
        return jnp.concatenate([half_turn(f), f], 0)

    sub10 = iota((16, 10), 0)
    block_of_row = 2 * (sub10 & 7) + (sub10 >> 3)
    live_row = jnp.sum(
        jnp.where(iota((16, 10), 1) == block_of_row, livev[...].astype(F32), 0.0), axis=1, keepdims=True
    )
    active = (lane16 & 63).astype(F32) < live_row
    wa, wb = planes(warm)
    wa, wb = jnp.where(active, wa, 0.0), jnp.where(active & low16, wb, 0.0)
    tab_send[0] = wa.astype(BF16)
    tab_send[1] = wb.astype(BF16)
    pl.semaphore_wait(bar, 38)
    send_body(tab_send, tab_recv.at[b], tab_s, tab_r)
    tab_recv[b] = tab_send[...]

    for cp in small[2:]:
        cp.wait()
    sa, sb = planes(step)
    con_send[0] = wa
    con_send[1] = jnp.where(low16, wb, jnp.where(active, high_plane(fric), -1.0))
    con_send[2] = sa
    con_send[3] = jnp.where(low16, sb, high_plane(bias))

    ids[0:1, :] = jnp.where(iota((1, 128), 1) < 32, 9999, 0)
    ids[1:2, :] = jnp.where(iota((1, 128), 1) < 32, 10000, 0)
    ids[0:1, 0:SLOTS] = rowv[...]
    ids[1:2, 0:SLOTS] = colv[...]
    lane1 = iota((1, 128), 1)
    row_l = ids[0:1, :]
    dev = (row_l * 52429) >> 19
    kk = row_l - 10 * dev
    place_l = jnp.where(
        lane1 < SLOTS, dev * 16 + (kk & 1) * 8 + (kk >> 1), jnp.where(lane1 < 32, 9999, 0)
    ).astype(F32)
    col_l = ids[1:2, :]
    owner_i = (col_l * 52429) >> 18
    within_l = (col_l - 5 * owner_i).astype(F32)
    owner_l = owner_i.astype(F32)

    sub32, lane32 = iota((32, 128), 0), iota((32, 128), 1)

    def down(v):
        return jnp.sum(jnp.where(sub32 == lane32, jnp.broadcast_to(v, (32, 128)), 0.0), axis=1, keepdims=True)

    place_s, owner_s, within_s = down(place_l), down(owner_l), down(within_l)
    rank_l = jnp.sum(
        jnp.where((owner_s == owner_l) & (sub32 < lane32) & (lane32 < 32), 1.0, 0.0), axis=0, keepdims=True
    )
    place8 = jnp.broadcast_to(place_l, (8, 128))
    con_send[4, 0:8, :] = pltpu.roll(jnp.where(lane8 < 16, place8, 0.0), b * 16, axis=1)
    con_send[4, 8:16, :] = pltpu.roll(jnp.where((lane8 >= 16) & (lane8 < 32), place8, 0.0), (b * 16 + 112) % 128, axis=1)

    def four_times(v):
        v = jnp.broadcast_to(v, (8, 128))
        v = v + pltpu.roll(v, 32, axis=1)
        return (v + pltpu.roll(v, 64, axis=1))[0:1]

    owner4, rank4 = four_times(owner_l), four_times(rank_l)
    sub = iota((320, 1), 0)
    o_row = jnp.where(sub < 256, sub >> 3, jnp.where(sub < 288, sub - 256, (sub - 288) ^ 18))
    m_row = jnp.where(sub < 256, sub & 7, 8)
    r_row = jnp.where(m_row < 3, 0, jnp.where(m_row < 6, 1, 2))
    c_row = m_row - 3 * r_row
    hit = (owner4 == o_row.astype(F32)) & (rank4 == r_row.astype(F32))
    for tile in range(2):
        q = (iota((1, 128), 1) >> 5) + 4 * tile
        cq = jnp.where(q < 3, q, jnp.where(q < 6, q - 3, -1))
        pick[:, tile * 128:(tile + 1) * 128] = jnp.where(hit & (cq == c_row), 1.0, 0.0).astype(BF16)
    sub96 = iota((96, 1), 0)
    c96 = (sub96 >> 5).astype(F32)
    place = jnp.full((32, 1), -1000.0, F32)
    for k, (dz, dy) in enumerate(NEAR + ((0, 0),)):
        near = moved(8 - dz, 4 - dy)
        place = jnp.where(owner_s == near.astype(F32), float(k * 32), place)
        place = jnp.where(owner_s == antipode(near).astype(F32), float(k * 32 + 16), place)
    target96 = jnp.concatenate([place + within_s] * 3, axis=0) + 5 * c96
    meta_send[...] = jnp.where(lane1 < SLOTS, owner_l * 16 + rank_l * 5 + within_l, 9999.0)
    gather_one[...] = jnp.where(iota((96, 512), 1).astype(F32) == target96, 1.0, 0.0).astype(BF16)
    own_s = (b * 16 + iota((16, 1), 0)).astype(F32)
    place48 = jnp.concatenate([place_s, own_s], axis=0)
    slot_one[...] = jnp.where(iota((48, 128), 1).astype(F32) == place48, 1.0, 0.0).astype(BF16)
    for n, src in enumerate((free, mass)):
        rows = [src[w, 0:1, i * 128:(i + 1) * 128] for i in range(3) for w in range(5)]
        home[0, n] = jnp.concatenate(rows + [jnp.zeros((1, 128), F32)], axis=0)

    con_recv[b] = con_send[...]

    pltpu.make_async_remote_copy(
        src_ref=home.at[0], dst_ref=home.at[1], send_sem=home_s, recv_sem=home_r,
        device_id={"cont": antipode(c)}, device_id_type=MESH,
    ).start()

    def send_meta(p):
        pltpu.make_async_remote_copy(
            src_ref=meta_send, dst_ref=meta_recv.at[c], send_sem=meta_s, recv_sem=meta_r,
            device_id={"cont": p}, device_id_type=MESH,
        ).start()

    over_cont(send_meta)
    meta_recv[c] = meta_send[...]

    drain(tab_recv.at[pl.ds(0, 7)], tab_r)
    imp_a[...] = mm(slot_one[...], tab_recv[:, 0].reshape(128, 128))
    imp_b[...] = mm(slot_one[...], tab_recv[:, 1].reshape(128, 128))
    for cp in blocks:
        cp.wait()

    low32 = lane32 < 64

    def forces():
        ya, yb = imp_a[0:32, :], imp_b[0:32, :]
        turned = half_turn(ya)
        pattern = jnp.concatenate(
            [ya, jnp.where(low32, yb, turned), jnp.where(low32, turned, half_turn(yb))], axis=1
        ).astype(BF16)
        halves = []
        row = iota((16, 768), 0)
        lane = iota((16, 768), 1) // 192
        for h in range(2):
            rep = jnp.concatenate([pattern[16 * h:16 * h + 16]] * 2, axis=1)
            acc = jnp.zeros((16, 384), F32)
            for g in range(0, 16, 4):
                s = 16 * h + g
                n = min(4, SLOTS - s)
                lhs = jnp.where(lane + g == row, rep, jnp.zeros_like(rep))[:, :n * 192]
                acc = acc + mm(lhs, jac[s:s + n].reshape(n * 192, 384))
            halves.append(acc)
        return jnp.concatenate(halves, axis=0)

    def locals_of(v, h):
        row = iota((16, 768), 0) // 2
        lane = iota((16, 768), 1) // 384
        rep = jnp.concatenate([v[16 * h:16 * h + 16]] * 2, axis=1)
        acc = jnp.zeros((16, 384), F32)
        for g in range(0, 8, 2):
            p = 8 * h + g
            n = min(2, SLOTS // 2 - p)
            lhs = jnp.where(lane + g == row, rep, jnp.zeros_like(rep))[:, :n * 384]
            acc = acc + mm(lhs, jact[p:p + n].reshape(n * 384, 384))
        return acc

    def sweep(t, carry):
        sf = forces()
        most = jnp.max(jnp.abs(sf), axis=0, keepdims=True)
        most = jnp.maximum(jnp.maximum(most[:, 0:128], most[:, 128:256]), most[:, 256:384])
        most = jnp.max(most, axis=1, keepdims=True)
        power = jnp.floor(jnp.log2(jnp.maximum(jnp.broadcast_to(most, (1, 128)), 1e-30))) + 1.0
        scale = jnp.exp2(15.0 - power)
        code = jnp.clip(jnp.round(sf * jnp.concatenate([scale] * 3, axis=1)), -32767.0, 32767.0)
        hi, mid = split(code)
        stacked = jnp.concatenate(
            [part[:, n * 128:(n + 1) * 128] for part in (hi, mid) for n in range(3)], axis=0
        )
        packed = mm(pick[:, 0:192], stacked).astype(I32)
        other = jnp.concatenate([packed[8 * (o ^ 18):8 * (o ^ 18) + 8] for o in range(32)], axis=0)
        force_send[t, :, 0:8, :] = (packed[0:256] * 65536 + other).reshape(32, 8, 128)
        force_send[t, :, 8:9, :] = (packed[256:288] * 65536 + packed[288:320]).reshape(32, 1, 128)
        force_send[t, :, 9:10, :] = jnp.broadcast_to(power.astype(I32).reshape(1, 1, 128), (32, 1, 128))

        def send_force(p):
            pltpu.make_async_remote_copy(
                src_ref=force_send.at[t, p], dst_ref=force_recv.at[t, c], send_sem=force_s.at[t],
                recv_sem=force_r.at[t], device_id={"cont": p}, device_id_type=MESH,
            ).start()

        over_cont(send_force)
        force_recv[t, c] = force_send[t, c]

        @pl.when(t == 0)
        def _():
            send_body(con_send, con_recv.at[b], con_s, con_r)
            drain(home.at[1], home_r)
            drain(meta_recv.at[pl.ds(0, 31)], meta_r)
            codes = meta_recv[...].reshape(32, 128)
            line = iota((32, 8, 128), 1)
            lane288 = iota((288, 128), 1).astype(F32)
            sub288 = iota((288, 128), 0)
            m288 = jnp.where(sub288 < 256, sub288 & 7, 8)
            col288 = (m288 - 3 * jnp.where(m288 < 3, 0, jnp.where(m288 < 6, 1, 2))).astype(F32)
            for role, h in enumerate((c, antipode(c))):
                rel = codes - (16 * h).astype(F32)
                found = []
                for r in range(3):
                    fits = (rel >= 5 * r) & (rel < 5 * r + 5)
                    one = jnp.sum(jnp.where(fits, rel - (5 * r - 1), 0.0), axis=1, keepdims=True)
                    found.append(jnp.broadcast_to(one, (32, 128)))
                wide = [jnp.broadcast_to(f.reshape(32, 1, 128), (32, 8, 128)) for f in found]
                rows = jnp.where(line < 3, wide[0], jnp.where(line < 6, wide[1], wide[2])).reshape(256, 128)
                rows = jnp.concatenate([rows, found[2]], axis=0)
                hits = (rows > 0.0) & (lane288 == rows - 1.0 + 5 * col288)
                meta = jnp.concatenate([jnp.where(hits, 1.0, 0.0), jnp.zeros((96, 128), F32)], axis=0)
                owner_one[role] = jnp.transpose(meta)[0:16].astype(BF16)
            for p in range(SLOTS // 2):
                jact[p] = jnp.transpose(jac[2 * p:2 * p + 2].reshape(384, 384))
            drain(con_recv.at[pl.ds(0, 7)], con_r)
            for h in range(2):
                got_ids = con_recv[0, 4, 8 * h:8 * h + 1, :]
                for d in range(1, 8):
                    got_ids = got_ids + con_recv[d, 4, 8 * h:8 * h + 1, :]
                row_one[:, h * 128:(h + 1) * 128] = jnp.where(got_ids == place48, 1.0, 0.0).astype(BF16)
            low48 = iota((48, 128), 1) < 64

            def exact(n):
                plane = con_recv[:, n].reshape(128, 128)
                p0, p1 = split(plane)
                p2 = (plane - p0.astype(F32) - p1.astype(F32)).astype(BF16)
                return mm(slot_one[...], p0) + (mm(slot_one[...], p1) + mm(slot_one[...], p2))

            imp_a[...] = exact(0)
            both = exact(1)
            imp_b[...] = jnp.where(low48, both, 0.0)
            fric48[...] = jnp.where(low48, half_turn(both), both)
            step_a[...] = exact(2)
            both = exact(3)
            step_b[...] = both
            shift48[...] = jnp.where(low48, half_turn(both), 0.0)

        @pl.when(t == SWEEPS)
        def _():
            own_a, own_b = imp_a[32:48, :], imp_b[32:48, :]
            ae, ao, be, bo = own_a[0:8], own_a[8:16], own_b[0:8], own_b[8:16]
            outs = (
                jnp.where(low8, ae, half_turn(ao)),
                jnp.where(low8, half_turn(ae), ao),
                jnp.where(low8, be, half_turn(bo)),
            )
            for i in range(3):
                for p in range(5):
                    out[i, 0:1, p * 128:(p + 1) * 128] = outs[i][p:p + 1]

            drain(tab_recv.at[pl.ds(0, 7)], tab_s)
            drain(con_recv.at[pl.ds(0, 7)], con_s)
            drain(meta_recv.at[pl.ds(0, 31)], meta_s)
            drain(home.at[1], home_s)
            for n in range(SWEEPS):
                drain(force_recv.at[n, pl.ds(0, 31)], force_s.at[n])
                drain(vel_recv.at[n, pl.ds(0, 15)], vel_s.at[n])
                for h in range(2):
                    drain(loc_recv.at[n, h, pl.ds(0, 7)], loc_s.at[n, h])

        drain(force_recv.at[t, pl.ds(0, 31)], force_r.at[t])
        word = jnp.concatenate(
            [force_recv[t, :, 0:8, :].reshape(256, 128), force_recv[t, :, 8:9, :].reshape(32, 128)], axis=0
        )
        unit = jnp.exp2(force_recv[t, :, 9:10, :].reshape(32, 128).astype(F32) - 15.0)
        units = jnp.concatenate(
            [jnp.broadcast_to(unit.reshape(32, 1, 128), (32, 8, 128)).reshape(256, 128), unit], axis=0
        )
        upper = (word + 32768) >> 16
        both_homes = []
        for role, value in enumerate((upper, word - (upper << 16))):
            parts = jnp.concatenate(split(value.astype(F32) * units), axis=1)
            force = mm(owner_one[role, :, 0:288], parts)
            force = force[:, 0:128] + force[:, 128:256]
            both_homes.append(home[role, 0] + home[role, 1] * force)
        velocity = both_homes[0]

        @pl.when(t == SWEEPS)
        def _():
            for n in range(3):
                for w in range(5):
                    i, p = divmod(w * 3 + n, 5)
                    out[3 + i, 0:1, p * 128:(p + 1) * 128] = velocity[n * 5 + w:n * 5 + w + 1]

        @pl.when(t < SWEEPS)
        def _():
            vel_send[t] = jnp.concatenate(both_homes, axis=0).astype(BF16)
            for k, (dz, dy) in enumerate(NEAR):
                pltpu.make_async_remote_copy(
                    src_ref=vel_send.at[t], dst_ref=vel_recv.at[t, k], send_sem=vel_s.at[t],
                    recv_sem=vel_r.at[t], device_id={"cont": moved(dz, dy)}, device_id_type=MESH,
                ).start()
            vel_recv[t, 15] = vel_send[t]
            drain(vel_recv.at[t, pl.ds(0, 15)], vel_r.at[t])
            vs = mm(gather_one[...], vel_recv[t].reshape(512, 128)).astype(BF16)
            v = jnp.concatenate([vs[0:32], vs[32:64], vs[64:96]], axis=1)
            even = (iota((16, 128), 0) & 1) == 0
            for h in range(2):
                loc = locals_of(v, h)
                l0, l1, l2 = loc[:, 0:128], loc[:, 128:256], loc[:, 256:384]
                t2 = half_turn(l2)
                la = jnp.where(even, l0, jnp.where(low16, half_turn(l1), t2))
                lb = jnp.where(even, l1, t2)
                ahi, amid = split(la)
                bhi = lb.astype(BF16).astype(F32)
                loc_send[t, h, 0] = ahi
                loc_send[t, h, 1] = amid
                loc_send[t, h, 2] = jnp.where(low16, bhi, half_turn(lb - bhi)).astype(BF16)
                send_body(loc_send.at[t, h], loc_recv.at[t, h, b], loc_s.at[t, h], loc_r.at[t, h])
                loc_recv[t, h, b] = loc_send[t, h]
            lv = jnp.zeros((48, 384), F32)
            for h in range(2):
                drain(loc_recv.at[t, h, pl.ds(0, 7)], loc_r.at[t, h])
                got_loc = jnp.concatenate([loc_recv[t, h, :, n].reshape(128, 128) for n in range(3)], axis=1)
                lv = lv + mm(row_one[:, h * 128:(h + 1) * 128], got_loc)
            lva = lv[:, 0:128] + lv[:, 128:256]
            lvb = lv[:, 256:384] + half_turn(lv[:, 256:384])
            low = iota((48, 128), 1) < 64
            fr = fric48[...]
            ta = imp_a[...] - step_a[...] * (lva + shift48[...])
            tb = imp_b[...] - step_b[...] * lvb
            normal = jnp.where(low, jnp.maximum(ta, 0.0), 0.0)
            lim_a = fr * half_turn(normal)
            lim_b = fr * normal
            live = fr >= 0.0
            new_a = jnp.where(low, normal, jnp.clip(ta, -lim_a, lim_a))
            imp_a[...] = jnp.where(live, new_a, 0.0)
            imp_b[...] = jnp.where(live & low, jnp.clip(tb, -lim_b, lim_b), 0.0)

        return carry

    lax.fori_loop(0, SWEEPS + 1, sweep, 0)

    drain(force_recv.at[SWEEPS, pl.ds(0, 31)], force_s.at[SWEEPS])


def shards(jacobian, row, col, live, warm, step, bias, fric, free, mass):
    dma = pltpu.SemaphoreType.DMA
    passes = SWEEPS + 1
    hbm = pl.BlockSpec(memory_space=pl.ANY)
    vmem = pl.BlockSpec(memory_space=pltpu.VMEM)
    out = pl.pallas_call(
        kernel,
        out_shape=jax.ShapeDtypeStruct((6, 1, 640), F32),
        in_specs=[hbm] * 10,
        out_specs=vmem,
        scratch_shapes=[
            pltpu.VMEM((SLOTS, 3, 64, 384), BF16),
            pltpu.VMEM((1, SLOTS), I32),
            pltpu.VMEM((1, SLOTS), I32),
            pltpu.VMEM((1, 10), I32),
            pltpu.VMEM((3, 1, 640), F32),
            pltpu.VMEM((3, 1, 640), F32),
            pltpu.VMEM((1, 640), F32),
            pltpu.VMEM((1, 640), F32),
            pltpu.VMEM((5, 1, 384), F32),
            pltpu.VMEM((5, 1, 384), F32),
            pltpu.VMEM((SLOTS // 2, 384, 384), BF16),
            pltpu.VMEM((8, 128), I32),
            pltpu.VMEM((320, 256), BF16),
            pltpu.VMEM((2, 16, 384), BF16),
            pltpu.VMEM((48, 128), BF16),
            pltpu.VMEM((48, 256), BF16),
            pltpu.VMEM((96, 512), BF16),
            pltpu.VMEM((48, 128), F32),
            pltpu.VMEM((48, 128), F32),
            pltpu.VMEM((48, 128), F32),
            pltpu.VMEM((48, 128), F32),
            pltpu.VMEM((48, 128), F32),
            pltpu.VMEM((48, 128), F32),
            pltpu.VMEM((2, 2, 16, 128), F32),
            pltpu.VMEM((2, 16, 128), BF16),
            pltpu.VMEM((8, 2, 16, 128), BF16),
            pltpu.VMEM((5, 16, 128), F32),
            pltpu.VMEM((8, 5, 16, 128), F32),
            pltpu.VMEM((1, 128), F32),
            pltpu.VMEM((32, 1, 128), F32),
            pltpu.VMEM((passes, 32, 10, 128), I32),
            pltpu.VMEM((passes, 32, 10, 128), I32),
            pltpu.VMEM((SWEEPS, 32, 128), BF16),
            pltpu.VMEM((SWEEPS, 16, 32, 128), BF16),
            pltpu.VMEM((SWEEPS, 2, 3, 16, 128), BF16),
            pltpu.VMEM((SWEEPS, 2, 8, 3, 16, 128), BF16),
            dma((5,)), dma((9,)), dma, dma, dma, dma, dma, dma, dma, dma,
            dma((passes,)), dma((passes,)), dma((SWEEPS,)), dma((SWEEPS,)), dma((SWEEPS, 2)), dma((SWEEPS, 2)),
        ],
        compiler_params=pltpu.CompilerParams(
            collective_id=0, has_side_effects=True, vmem_limit_bytes=32 << 20
        ),
        name="sweeps",
    )(*[
        pltpu.with_memory_space_constraint(v, pltpu.HBM)
        for v in (
            jacobian.reshape(jacobian.shape[1:]), row, col, live, warm, step, bias, fric,
            free.transpose(1, 0, 2), mass.transpose(1, 0, 2),
        )
    ])
    return out[0:3], out[3:6].reshape(5, 1, 384).transpose(1, 0, 2)


def solution(mesh):
    placed = (
        P("body", "cont", None, None, None),
        P("body", "cont"),
        P("body", "cont"),
        P("cont", "body"),
        P(None, "cont", "body"),
        P(None, "cont", "body"),
        P("cont", "body"),
        P("cont", "body"),
        P("body", "cont", None),
        P("body", "cont", None),
    )
    return jax.shard_map(
        shards,
        mesh=mesh,
        in_specs=placed,
        out_specs=(P(None, "cont", "body"), P("body", "cont", None)),
        check_vma=False,
    )
```

```python
import jax
import jax.numpy as jnp
from jax import lax
from jax.experimental import pallas as pl
from jax.experimental.pallas import tpu as pltpu
from jax.sharding import PartitionSpec as P

MESH = pl.DeviceIdType.MESH
SWEEPS = 3
SLOTS = 30
NEAR = (
    (1, 2), (7, 2), (2, 1), (6, 1), (2, 0), (6, 0), (1, 1), (1, 3), (7, 1), (7, 3), (0, 2),
    (1, 0), (7, 0), (0, 1), (0, 3),
)
FAR_FIRST = tuple(sorted(
    ((dz, dy) for dz in (4, 3, 5, 2, 6, 1, 7, 0) for dy in (2, 1, 3, 0) if (dz, dy) != (0, 0)),
    key=lambda step: -min(step[0], 8 - step[0]) - min(step[1], 4 - step[1]),
))
F32, BF16, I32 = jnp.float32, jnp.bfloat16, jnp.int32


def iota(shape, dim):
    return lax.broadcasted_iota(I32, shape, dim)


def half_turn(x):
    return pltpu.roll(x, 64, axis=x.ndim - 1)


def split(x):
    hi = x.astype(BF16)
    mid = (x - hi.astype(F32)).astype(BF16)
    return hi, mid


def mm(a, b):
    return jnp.dot(a, b, preferred_element_type=F32)


def kernel(
    jac_in, row_in, col_in, live_in, warm_in, step_in, bias_in, fric_in, free_in, mass_in,
    out,
    jac, rowv, colv, livev, warm, step, bias, fric, free, mass,
    jact, ids, pick, owner_one, slot_one, row_one, gather_one,
    imp_a, imp_b, step_a, step_b, fric48, shift48, home,
    tab_send, tab_recv, con_send, con_recv, meta_send, meta_recv,
    force_send, force_recv, vel_send, vel_recv, loc_send, loc_recv,
    jac_sem, in_sem, home_s, home_r, tab_s, tab_r, con_s, con_r, meta_s, meta_r,
    force_s, force_r, vel_s, vel_r, loc_s, loc_r,
):
    b, c = lax.axis_index("body"), lax.axis_index("cont")
    x, core, z, y = b // 2, b % 2, c // 4, c % 4

    def moved(dz, dy):
        return ((z + dz) % 8) * 4 + (y + dy) % 4

    def antipode(p):
        return ((p // 4 + 4) % 8) * 4 + (p % 4 + 2) % 4

    body_peers = [
        ((x + dx) % 4) * 2 + (core + dc) % 2
        for dx, dc in ((2, 1), (2, 0), (1, 1), (3, 1), (1, 0), (3, 0), (0, 1))
    ]

    def over_cont(go):
        for dz, dy in FAR_FIRST:
            go(moved(dz, dy))

    def send_body(src, dst, ssem, rsem):
        for p in body_peers:
            pltpu.make_async_remote_copy(
                src_ref=src, dst_ref=dst, send_sem=ssem, recv_sem=rsem,
                device_id={"body": p}, device_id_type=MESH,
            ).start()

    def drain(ref, sem):
        pltpu.make_async_copy(ref, ref, sem).wait()

    bar = pltpu.get_barrier_semaphore()
    over_cont(lambda p: pl.semaphore_signal(bar, inc=1, device_id={"cont": p}, device_id_type=MESH))
    for p in body_peers:
        pl.semaphore_signal(bar, inc=1, device_id={"body": p}, device_id_type=MESH)

    pairs = (
        (warm_in, warm), (live_in, livev), (row_in, rowv), (col_in, colv), (step_in, step),
        (bias_in, bias), (fric_in, fric), (free_in, free), (mass_in, mass),
    )
    small = [pltpu.make_async_copy(s, d, in_sem.at[n]) for n, (s, d) in enumerate(pairs)]
    for cp in small:
        cp.start()
    blocks = [
        pltpu.make_async_copy(jac_in.at[pl.ds(n * 6, 6)], jac.at[pl.ds(n * 6, 6)], jac_sem.at[n])
        for n in range(5)
    ]
    for cp in blocks:
        cp.start()
    for cp in small[:2]:
        cp.wait()

    lane16 = iota((16, 128), 1)
    low16 = lane16 < 64
    lane8 = iota((8, 128), 1)
    low8 = lane8 < 64

    def rows_of(get):
        parts = [get(p).astype(F32) for p in range(5)]
        return jnp.concatenate(parts + [jnp.zeros((3, 128), F32)], axis=0)

    def planes(ref):
        w0, w1, w2 = [rows_of(lambda p, i=i: ref[i, 0:1, p * 128:(p + 1) * 128]) for i in range(3)]
        even = jnp.where(low8, w0, half_turn(w1))
        odd = jnp.where(low8, half_turn(w0), w1)
        return jnp.concatenate([even, odd], 0), jnp.concatenate([w2, half_turn(w2)], 0)

    def high_plane(ref):
        f = rows_of(lambda p: ref[0:1, p * 128:(p + 1) * 128])
        return jnp.concatenate([half_turn(f), f], 0)

    sub10 = iota((16, 10), 0)
    block_of_row = 2 * (sub10 & 7) + (sub10 >> 3)
    live_row = jnp.sum(
        jnp.where(iota((16, 10), 1) == block_of_row, livev[...].astype(F32), 0.0), axis=1, keepdims=True
    )
    active = (lane16 & 63).astype(F32) < live_row
    wa, wb = planes(warm)
    wa, wb = jnp.where(active, wa, 0.0), jnp.where(active & low16, wb, 0.0)
    tab_send[0] = wa.astype(BF16)
    tab_send[1] = wb.astype(BF16)
    pl.semaphore_wait(bar, 38)
    send_body(tab_send, tab_recv.at[b], tab_s, tab_r)
    tab_recv[b] = tab_send[...]

    for cp in small[2:]:
        cp.wait()
    sa, sb = planes(step)
    con_send[0] = wa
    con_send[1] = jnp.where(low16, wb, jnp.where(active, high_plane(fric), -1.0))
    con_send[2] = sa
    con_send[3] = jnp.where(low16, sb, high_plane(bias))

    ids[0:1, :] = jnp.where(iota((1, 128), 1) < 32, 9999, 0)
    ids[1:2, :] = jnp.where(iota((1, 128), 1) < 32, 10000, 0)
    ids[0:1, 0:SLOTS] = rowv[...]
    ids[1:2, 0:SLOTS] = colv[...]
    lane1 = iota((1, 128), 1)
    row_l = ids[0:1, :]
    dev = (row_l * 52429) >> 19
    kk = row_l - 10 * dev
    place_l = jnp.where(
        lane1 < SLOTS, dev * 16 + (kk & 1) * 8 + (kk >> 1), jnp.where(lane1 < 32, 9999, 0)
    ).astype(F32)
    col_l = ids[1:2, :]
    owner_i = (col_l * 52429) >> 18
    within_l = (col_l - 5 * owner_i).astype(F32)
    owner_l = owner_i.astype(F32)

    sub32, lane32 = iota((32, 128), 0), iota((32, 128), 1)

    def down(v):
        return jnp.sum(jnp.where(sub32 == lane32, jnp.broadcast_to(v, (32, 128)), 0.0), axis=1, keepdims=True)

    place_s, owner_s, within_s = down(place_l), down(owner_l), down(within_l)
    rank_l = jnp.sum(
        jnp.where((owner_s == owner_l) & (sub32 < lane32) & (lane32 < 32), 1.0, 0.0), axis=0, keepdims=True
    )
    place8 = jnp.broadcast_to(place_l, (8, 128))
    con_send[4, 0:8, :] = pltpu.roll(jnp.where(lane8 < 16, place8, 0.0), b * 16, axis=1)
    con_send[4, 8:16, :] = pltpu.roll(jnp.where((lane8 >= 16) & (lane8 < 32), place8, 0.0), (b * 16 + 112) % 128, axis=1)

    def four_times(v):
        v = jnp.broadcast_to(v, (8, 128))
        v = v + pltpu.roll(v, 32, axis=1)
        return (v + pltpu.roll(v, 64, axis=1))[0:1]

    owner4, rank4 = four_times(owner_l), four_times(rank_l)
    sub = iota((320, 1), 0)
    o_row = jnp.where(sub < 256, sub >> 3, jnp.where(sub < 288, sub - 256, (sub - 288) ^ 18))
    m_row = jnp.where(sub < 256, sub & 7, 8)
    r_row = jnp.where(m_row < 3, 0, jnp.where(m_row < 6, 1, 2))
    c_row = m_row - 3 * r_row
    hit = (owner4 == o_row.astype(F32)) & (rank4 == r_row.astype(F32))
    for tile in range(2):
        q = (iota((1, 128), 1) >> 5) + 4 * tile
        cq = jnp.where(q < 3, q, jnp.where(q < 6, q - 3, -1))
        pick[:, tile * 128:(tile + 1) * 128] = jnp.where(hit & (cq == c_row), 1.0, 0.0).astype(BF16)
    sub96 = iota((96, 1), 0)
    c96 = (sub96 >> 5).astype(F32)
    place = jnp.full((32, 1), -1000.0, F32)
    for k, (dz, dy) in enumerate(NEAR + ((0, 0),)):
        near = moved(8 - dz, 4 - dy)
        place = jnp.where(owner_s == near.astype(F32), float(k * 32), place)
        place = jnp.where(owner_s == antipode(near).astype(F32), float(k * 32 + 16), place)
    target96 = jnp.concatenate([place + within_s] * 3, axis=0) + 5 * c96
    meta_send[...] = jnp.where(lane1 < SLOTS, owner_l * 16 + rank_l * 5 + within_l, 9999.0)
    gather_one[...] = jnp.where(iota((96, 512), 1).astype(F32) == target96, 1.0, 0.0).astype(BF16)
    own_s = (b * 16 + iota((16, 1), 0)).astype(F32)
    place48 = jnp.concatenate([place_s, own_s], axis=0)
    slot_one[...] = jnp.where(iota((48, 128), 1).astype(F32) == place48, 1.0, 0.0).astype(BF16)
    for n, src in enumerate((free, mass)):
        rows = [src[w, 0:1, i * 128:(i + 1) * 128] for i in range(3) for w in range(5)]
        home[0, n] = jnp.concatenate(rows + [jnp.zeros((1, 128), F32)], axis=0)

    con_recv[b] = con_send[...]

    pltpu.make_async_remote_copy(
        src_ref=home.at[0], dst_ref=home.at[1], send_sem=home_s, recv_sem=home_r,
        device_id={"cont": antipode(c)}, device_id_type=MESH,
    ).start()

    def send_meta(p):
        pltpu.make_async_remote_copy(
            src_ref=meta_send, dst_ref=meta_recv.at[c], send_sem=meta_s, recv_sem=meta_r,
            device_id={"cont": p}, device_id_type=MESH,
        ).start()

    over_cont(send_meta)
    meta_recv[c] = meta_send[...]

    drain(tab_recv.at[pl.ds(0, 7)], tab_r)
    imp_a[...] = mm(slot_one[...], tab_recv[:, 0].reshape(128, 128))
    imp_b[...] = mm(slot_one[...], tab_recv[:, 1].reshape(128, 128))
    for cp in blocks:
        cp.wait()

    low32 = lane32 < 64

    def forces():
        ya, yb = imp_a[0:32, :], imp_b[0:32, :]
        turned = half_turn(ya)
        pattern = jnp.concatenate(
            [ya, jnp.where(low32, yb, turned), jnp.where(low32, turned, half_turn(yb))], axis=1
        ).astype(BF16)
        halves = []
        row = iota((16, 768), 0)
        lane = iota((16, 768), 1) // 192
        for h in range(2):
            rep = jnp.concatenate([pattern[16 * h:16 * h + 16]] * 2, axis=1)
            acc = jnp.zeros((16, 384), F32)
            for g in range(0, 16, 4):
                s = 16 * h + g
                n = min(4, SLOTS - s)
                lhs = jnp.where(lane + g == row, rep, jnp.zeros_like(rep))[:, :n * 192]
                acc = acc + mm(lhs, jac[s:s + n].reshape(n * 192, 384))
            halves.append(acc)
        return jnp.concatenate(halves, axis=0)

    def locals_of(v, h):
        row = iota((16, 768), 0) // 2
        lane = iota((16, 768), 1) // 384
        rep = jnp.concatenate([v[16 * h:16 * h + 16]] * 2, axis=1)
        acc = jnp.zeros((16, 384), F32)
        for g in range(0, 8, 2):
            p = 8 * h + g
            n = min(2, SLOTS // 2 - p)
            lhs = jnp.where(lane + g == row, rep, jnp.zeros_like(rep))[:, :n * 384]
            acc = acc + mm(lhs, jact[p:p + n].reshape(n * 384, 384))
        return acc

    def sweep(t, carry):
        sf = forces()
        most = jnp.max(jnp.abs(sf), axis=0, keepdims=True)
        most = jnp.maximum(jnp.maximum(most[:, 0:128], most[:, 128:256]), most[:, 256:384])
        most = jnp.max(most, axis=1, keepdims=True)
        power = jnp.floor(jnp.log2(jnp.maximum(jnp.broadcast_to(most, (1, 128)), 1e-30))) + 1.0
        scale = jnp.exp2(15.0 - power)
        code = jnp.clip(jnp.round(sf * jnp.concatenate([scale] * 3, axis=1)), -32767.0, 32767.0)
        hi, mid = split(code)
        stacked = jnp.concatenate(
            [part[:, n * 128:(n + 1) * 128] for part in (hi, mid) for n in range(3)], axis=0
        )
        packed = mm(pick[:, 0:192], stacked).astype(I32)
        other = jnp.concatenate([packed[8 * (o ^ 18):8 * (o ^ 18) + 8] for o in range(32)], axis=0)
        force_send[t, :, 0:8, :] = (packed[0:256] * 65536 + other).reshape(32, 8, 128)
        force_send[t, :, 8:9, :] = (packed[256:288] * 65536 + packed[288:320]).reshape(32, 1, 128)
        force_send[t, :, 9:10, :] = jnp.broadcast_to(power.astype(I32).reshape(1, 1, 128), (32, 1, 128))

        def send_force(p):
            pltpu.make_async_remote_copy(
                src_ref=force_send.at[t, p], dst_ref=force_recv.at[t, c], send_sem=force_s.at[t],
                recv_sem=force_r.at[t], device_id={"cont": p}, device_id_type=MESH,
            ).start()

        over_cont(send_force)
        force_recv[t, c] = force_send[t, c]

        @pl.when(t == 0)
        def _():
            send_body(con_send, con_recv.at[b], con_s, con_r)
            drain(home.at[1], home_r)
            drain(meta_recv.at[pl.ds(0, 31)], meta_r)
            codes = meta_recv[...].reshape(32, 128)
            line = iota((32, 8, 128), 1)
            lane288 = iota((288, 128), 1).astype(F32)
            sub288 = iota((288, 128), 0)
            m288 = jnp.where(sub288 < 256, sub288 & 7, 8)
            col288 = (m288 - 3 * jnp.where(m288 < 3, 0, jnp.where(m288 < 6, 1, 2))).astype(F32)
            for role, h in enumerate((c, antipode(c))):
                rel = codes - (16 * h).astype(F32)
                found = []
                for r in range(3):
                    fits = (rel >= 5 * r) & (rel < 5 * r + 5)
                    one = jnp.sum(jnp.where(fits, rel - (5 * r - 1), 0.0), axis=1, keepdims=True)
                    found.append(jnp.broadcast_to(one, (32, 128)))
                wide = [jnp.broadcast_to(f.reshape(32, 1, 128), (32, 8, 128)) for f in found]
                rows = jnp.where(line < 3, wide[0], jnp.where(line < 6, wide[1], wide[2])).reshape(256, 128)
                rows = jnp.concatenate([rows, found[2]], axis=0)
                hits = (rows > 0.0) & (lane288 == rows - 1.0 + 5 * col288)
                meta = jnp.concatenate([jnp.where(hits, 1.0, 0.0), jnp.zeros((96, 128), F32)], axis=0)
                owner_one[role] = jnp.transpose(meta)[0:16].astype(BF16)
            for p in range(SLOTS // 2):
                jact[p] = jnp.transpose(jac[2 * p:2 * p + 2].reshape(384, 384))
            drain(con_recv.at[pl.ds(0, 7)], con_r)
            for h in range(2):
                got_ids = con_recv[0, 4, 8 * h:8 * h + 1, :]
                for d in range(1, 8):
                    got_ids = got_ids + con_recv[d, 4, 8 * h:8 * h + 1, :]
                row_one[:, h * 128:(h + 1) * 128] = jnp.where(got_ids == place48, 1.0, 0.0).astype(BF16)
            low48 = iota((48, 128), 1) < 64

            def exact(n):
                plane = con_recv[:, n].reshape(128, 128)
                p0, p1 = split(plane)
                p2 = (plane - p0.astype(F32) - p1.astype(F32)).astype(BF16)
                return mm(slot_one[...], p0) + (mm(slot_one[...], p1) + mm(slot_one[...], p2))

            imp_a[...] = exact(0)
            both = exact(1)
            imp_b[...] = jnp.where(low48, both, 0.0)
            fric48[...] = jnp.where(low48, half_turn(both), both)
            step_a[...] = exact(2)
            both = exact(3)
            step_b[...] = both
            shift48[...] = jnp.where(low48, half_turn(both), 0.0)

        @pl.when(t == SWEEPS)
        def _():
            own_a, own_b = imp_a[32:48, :], imp_b[32:48, :]
            ae, ao, be, bo = own_a[0:8], own_a[8:16], own_b[0:8], own_b[8:16]
            outs = (
                jnp.where(low8, ae, half_turn(ao)),
                jnp.where(low8, half_turn(ae), ao),
                jnp.where(low8, be, half_turn(bo)),
            )
            for i in range(3):
                for p in range(5):
                    out[i, 0:1, p * 128:(p + 1) * 128] = outs[i][p:p + 1]

            drain(tab_recv.at[pl.ds(0, 7)], tab_s)
            drain(con_recv.at[pl.ds(0, 7)], con_s)
            drain(meta_recv.at[pl.ds(0, 31)], meta_s)
            drain(home.at[1], home_s)
            for n in range(SWEEPS):
                drain(force_recv.at[n, pl.ds(0, 31)], force_s.at[n])
                drain(vel_recv.at[n, pl.ds(0, 15)], vel_s.at[n])
                for h in range(2):
                    drain(loc_recv.at[n, h, pl.ds(0, 7)], loc_s.at[n, h])

        drain(force_recv.at[t, pl.ds(0, 31)], force_r.at[t])
        word = jnp.concatenate(
            [force_recv[t, :, 0:8, :].reshape(256, 128), force_recv[t, :, 8:9, :].reshape(32, 128)], axis=0
        )
        unit = jnp.exp2(force_recv[t, :, 9:10, :].reshape(32, 128).astype(F32) - 15.0)
        units = jnp.concatenate(
            [jnp.broadcast_to(unit.reshape(32, 1, 128), (32, 8, 128)).reshape(256, 128), unit], axis=0
        )
        upper = (word + 32768) >> 16
        both_homes = []
        for role, value in enumerate((upper, word - (upper << 16))):
            parts = jnp.concatenate(split(value.astype(F32) * units), axis=1)
            force = mm(owner_one[role, :, 0:288], parts)
            force = force[:, 0:128] + force[:, 128:256]
            both_homes.append(home[role, 0] + home[role, 1] * force)
        velocity = both_homes[0]

        @pl.when(t == SWEEPS)
        def _():
            for n in range(3):
                for w in range(5):
                    i, p = divmod(w * 3 + n, 5)
                    out[3 + i, 0:1, p * 128:(p + 1) * 128] = velocity[n * 5 + w:n * 5 + w + 1]

        @pl.when(t < SWEEPS)
        def _():
            vel_send[t] = jnp.concatenate(both_homes, axis=0).astype(BF16)
            for k, (dz, dy) in enumerate(NEAR):
                pltpu.make_async_remote_copy(
                    src_ref=vel_send.at[t], dst_ref=vel_recv.at[t, k], send_sem=vel_s.at[t],
                    recv_sem=vel_r.at[t], device_id={"cont": moved(dz, dy)}, device_id_type=MESH,
                ).start()
            vel_recv[t, 15] = vel_send[t]
            drain(vel_recv.at[t, pl.ds(0, 15)], vel_r.at[t])
            vs = mm(gather_one[...], vel_recv[t].reshape(512, 128)).astype(BF16)
            v = jnp.concatenate([vs[0:32], vs[32:64], vs[64:96]], axis=1)
            even = (iota((16, 128), 0) & 1) == 0
            for h in range(2):
                loc = locals_of(v, h)
                l0, l1, l2 = loc[:, 0:128], loc[:, 128:256], loc[:, 256:384]
                t2 = half_turn(l2)
                la = jnp.where(even, l0, jnp.where(low16, half_turn(l1), t2))
                lb = jnp.where(even, l1, t2)
                ahi, amid = split(la)
                bhi = lb.astype(BF16).astype(F32)
                loc_send[t, h, 0] = ahi
                loc_send[t, h, 1] = amid
                loc_send[t, h, 2] = jnp.where(low16, bhi, half_turn(lb - bhi)).astype(BF16)
                send_body(loc_send.at[t, h], loc_recv.at[t, h, b], loc_s.at[t, h], loc_r.at[t, h])
                loc_recv[t, h, b] = loc_send[t, h]
            lv = jnp.zeros((48, 384), F32)
            for h in range(2):
                drain(loc_recv.at[t, h, pl.ds(0, 7)], loc_r.at[t, h])
                got_loc = jnp.concatenate([loc_recv[t, h, :, n].reshape(128, 128) for n in range(3)], axis=1)
                lv = lv + mm(row_one[:, h * 128:(h + 1) * 128], got_loc)
            lva = lv[:, 0:128] + lv[:, 128:256]
            lvb = lv[:, 256:384] + half_turn(lv[:, 256:384])
            low = iota((48, 128), 1) < 64
            fr = fric48[...]
            ta = imp_a[...] - step_a[...] * (lva + shift48[...])
            tb = imp_b[...] - step_b[...] * lvb
            normal = jnp.where(low, jnp.maximum(ta, 0.0), 0.0)
            lim_a = fr * half_turn(normal)
            lim_b = fr * normal
            live = fr >= 0.0
            new_a = jnp.where(low, normal, jnp.clip(ta, -lim_a, lim_a))
            imp_a[...] = jnp.where(live, new_a, 0.0)
            imp_b[...] = jnp.where(live & low, jnp.clip(tb, -lim_b, lim_b), 0.0)

        return carry

    lax.fori_loop(0, SWEEPS + 1, sweep, 0)

    drain(force_recv.at[SWEEPS, pl.ds(0, 31)], force_s.at[SWEEPS])


def shards(jacobian, row, col, live, warm, step, bias, fric, free, mass):
    dma = pltpu.SemaphoreType.DMA
    passes = SWEEPS + 1
    hbm = pl.BlockSpec(memory_space=pl.ANY)
    vmem = pl.BlockSpec(memory_space=pltpu.VMEM)
    out = pl.pallas_call(
        kernel,
        out_shape=jax.ShapeDtypeStruct((6, 1, 640), F32),
        in_specs=[hbm] * 10,
        out_specs=vmem,
        scratch_shapes=[
            pltpu.VMEM((SLOTS, 3, 64, 384), BF16),
            pltpu.VMEM((1, SLOTS), I32),
            pltpu.VMEM((1, SLOTS), I32),
            pltpu.VMEM((1, 10), I32),
            pltpu.VMEM((3, 1, 640), F32),
            pltpu.VMEM((3, 1, 640), F32),
            pltpu.VMEM((1, 640), F32),
            pltpu.VMEM((1, 640), F32),
            pltpu.VMEM((5, 1, 384), F32),
            pltpu.VMEM((5, 1, 384), F32),
            pltpu.VMEM((SLOTS // 2, 384, 384), BF16),
            pltpu.VMEM((8, 128), I32),
            pltpu.VMEM((320, 256), BF16),
            pltpu.VMEM((2, 16, 384), BF16),
            pltpu.VMEM((48, 128), BF16),
            pltpu.VMEM((48, 256), BF16),
            pltpu.VMEM((96, 512), BF16),
            pltpu.VMEM((48, 128), F32),
            pltpu.VMEM((48, 128), F32),
            pltpu.VMEM((48, 128), F32),
            pltpu.VMEM((48, 128), F32),
            pltpu.VMEM((48, 128), F32),
            pltpu.VMEM((48, 128), F32),
            pltpu.VMEM((2, 2, 16, 128), F32),
            pltpu.VMEM((2, 16, 128), BF16),
            pltpu.VMEM((8, 2, 16, 128), BF16),
            pltpu.VMEM((5, 16, 128), F32),
            pltpu.VMEM((8, 5, 16, 128), F32),
            pltpu.VMEM((1, 128), F32),
            pltpu.VMEM((32, 1, 128), F32),
            pltpu.VMEM((passes, 32, 10, 128), I32),
            pltpu.VMEM((passes, 32, 10, 128), I32),
            pltpu.VMEM((SWEEPS, 32, 128), BF16),
            pltpu.VMEM((SWEEPS, 16, 32, 128), BF16),
            pltpu.VMEM((SWEEPS, 2, 3, 16, 128), BF16),
            pltpu.VMEM((SWEEPS, 2, 8, 3, 16, 128), BF16),
            dma((5,)), dma((9,)), dma, dma, dma, dma, dma, dma, dma, dma,
            dma((passes,)), dma((passes,)), dma((SWEEPS,)), dma((SWEEPS,)), dma((SWEEPS, 2)), dma((SWEEPS, 2)),
        ],
        compiler_params=pltpu.CompilerParams(
            collective_id=0, has_side_effects=True, vmem_limit_bytes=32 << 20
        ),
        name="sweeps",
    )(*[
        pltpu.with_memory_space_constraint(v, pltpu.HBM)
        for v in (
            jacobian.reshape(jacobian.shape[1:]), row, col, live, warm, step, bias, fric,
            free.transpose(1, 0, 2), mass.transpose(1, 0, 2),
        )
    ])
    return out[0:3], out[3:6].reshape(5, 1, 384).transpose(1, 0, 2)


def solution(mesh):
    placed = (
        P("body", "cont", None, None, None),
        P("body", "cont"),
        P("body", "cont"),
        P("cont", "body"),
        P(None, "cont", "body"),
        P(None, "cont", "body"),
        P("cont", "body"),
        P("cont", "body"),
        P("body", "cont", None),
        P("body", "cont", None),
    )
    return jax.shard_map(
        shards,
        mesh=mesh,
        in_specs=placed,
        out_specs=(P(None, "cont", "body"), P("body", "cont", None)),
        check_vma=False,
    )
```
